32 devices in a mesh: groups: 2 (over x), inst: 4 (over y, core), tp: 4 (over z).
Axes of the slice: x: 2, y: 2, z: 4, core: 2. Of those that a mesh axis runs over, the one named last changes fastest.
Arguments:
- x_new: bfloat16 [2, 384, 16384], P(None, ('groups', 'inst'), 'tp'), parts along dimension 1, may hold values from -6 to 6
- z_new: bfloat16 [2, 384, 16384], P(None, ('groups', 'inst'), 'tp'), parts along dimension 1, may hold values from -6 to 6
- ssm_state: bfloat16 [384, 16, 16384], P(('groups', 'inst'), None, 'tp'), parts along dimension 0, may hold values from -4 to 4
- conv_state: bfloat16 [384, 3, 16384], P(('groups', 'inst'), None, 'tp'), parts along dimension 0, may hold values from -6 to 6
- conv_weight: float32 [4, 16384], P(None, 'tp'), may hold values from -3 to 3
- conv_bias: float32 [16384], P('tp'), may hold values from -0.5 to 0.5
- proj_weight: bfloat16 [16384, 544], P('tp'), may hold values from -1.5 to 1.5
- dt_weight: bfloat16 [512, 16384], P(None, 'tp'), may hold values from -0.25 to 0.25
- dt_bias: float32 [16384], P('tp'), may hold values from -6 to -1
- a_log: float32 [16, 16384], P(None, 'tp'), may hold values from 0 to 2.77
- skip_gain: float32 [16384], P('tp'), may hold values from 0.5 to 2
- leave_slot: int32 [8, 12], P(('groups', 'inst')), parts along dimension 0, may hold values from 0 to 47, as said below
- dest_table: int32 [8, 12], P('groups'), parts along dimension 0, may hold values from 0 to 3, as said below
- land_slot: int32 [8, 12], P(('groups', 'inst')), parts along dimension 0, may hold values from 0 to 47, as said below
Outputs:
- outputs: bfloat16 [2, 384, 16384], P(None, ('groups', 'inst'), 'tp'), parts along dimension 1
- new_ssm: bfloat16 [384, 16, 16384], P(('groups', 'inst'), None, 'tp'), parts along dimension 0
- new_conv: bfloat16 [384, 3, 16384], P(('groups', 'inst'), None, 'tp'), parts along dimension 0
The draws below stay inside these ranges and needn't reach their ends.
There are 2 independent parts, one for each index of `groups`. The reference program is written for one: setup_inputs(seed, part) draws one part's arguments, and reference() takes and returns one part's arrays. A program takes and returns all parts, laid end to end along the dimension named above; an argument that names none is the same for every part. Nothing has to cross between parts.
Inputs may be any that keep to these rules, and one draw needn't show every extreme that they name: `leave_slot`: each row holds 12 distinct slots. dest_table[i, k] is never i; every instance receives exactly 12 requests; no instance sends more than 4 to one destination, and every instance sends exactly 4 to some destination. `land_slot`: row j is a reordering of row j of leave_slot.
All inputs are finite; a program needn't handle non-finite values.
Results may differ from the reference program's by a relative error of at most 0.0056.
Values may be sent and summed in bfloat16 or wider, within the bound.
No kernel may reach another device: no remote copies, remote signals or barrier semaphores. Data moves between devices by JAX's collectives and lax.ppermute only.
A program may use at most 128 MiB of HBM per device.

```python
import math
import jax
import jax.numpy as jnp
from jax import lax

DI = 16384
NS = 16
RANK = 512
CONV_WIDTH = 4
STEPS = 2
SLOTS = 48
MIG = 12
CAP = 4
INSTANCES = 4
ROWS = 192


def pick_slots(row_key):
    return jax.random.permutation(row_key, SLOTS)[:MIG].astype(jnp.int32)


def shuffle_order(row_key):
    return jax.random.permutation(row_key, MIG).astype(jnp.int32)


def leaving_slots(key):
    key = jax.random.fold_in(key, 11)
    row_keys = jax.random.split(key, INSTANCES)
    return jax.vmap(pick_slots)(row_keys)


def draw_leave_slot(key, part):
    return leaving_slots(key)


def draw_land_slot(key, part):
    shared = leaving_slots(key)
    key = jax.random.fold_in(key, 5)
    row_keys = jax.random.split(key, INSTANCES)
    order_rows = jax.vmap(shuffle_order)(row_keys)
    return jnp.take_along_axis(shared, order_rows, axis=1).astype(jnp.int32)


def draw_dest_table(key, part):
    key = jax.random.fold_in(key, 2)
    key_shift, key_order = jax.random.split(key)
    half = INSTANCES // 2
    ordering = jax.random.permutation(key_shift, INSTANCES - 1).astype(jnp.int32)
    zero_at = jnp.argmax((ordering == 0).astype(jnp.int32)).astype(jnp.int32)
    ordering = ordering.at[zero_at].set(ordering[0]).at[0].set(0)
    values = jnp.arange(INSTANCES - 1, dtype=jnp.int32)
    shift_list = jnp.where(values == 0, half, jnp.where(values < half, values, values + 1)).astype(jnp.int32)
    blocks = (MIG + CAP - 1) // CAP
    chosen = shift_list[ordering[:blocks]]
    shifts = chosen[jnp.arange(MIG, dtype=jnp.int32) // CAP]
    row_keys = jax.random.split(key_order, INSTANCES)
    order_rows = jax.vmap(shuffle_order)(row_keys)
    shuffled = shifts[order_rows]
    sources = jnp.arange(INSTANCES, dtype=jnp.int32)[:, None]
    return ((sources + shuffled) % INSTANCES).astype(jnp.int32)


def draw_proj_weight(key, part):
    key = jax.random.fold_in(key, 7)
    key_base, key_scale = jax.random.split(key)
    columns = RANK + 2 * NS
    noise = jnp.clip(jax.random.normal(key_base, (DI, columns), jnp.float32), -4.0, 4.0)
    col_scale = jnp.exp(jax.random.uniform(key_scale, (1, columns), jnp.float32, math.log(0.5), math.log(5.0)))
    return (noise * col_scale * DI ** (-0.5)).astype(jnp.bfloat16)


def block_scale(key, dims, cuts, least, largest):
    def one(dim, blocks):
        steps = jax.random.uniform(jax.random.fold_in(jax.random.fold_in(key, 6), dim), (blocks,), jnp.float32, least / len(cuts), largest / len(cuts))
        return jnp.repeat(jnp.exp(steps), dims[dim] // blocks).reshape((-1,) + (1,) * (len(dims) - dim - 1))

    factor_of = one(*cuts[0])
    for cut in cuts[1:]:
        factor_of = factor_of * one(*cut)
    return factor_of


def scatter_about(stream_key, shape, scale, bound, cuts=(), kind=jnp.bfloat16):
    entries = scale * jax.random.normal(stream_key, shape, jnp.float32)
    if cuts:
        entries = entries * block_scale(stream_key, shape, cuts, -0.22, 0.18)
    return jnp.clip(entries, -bound, bound).astype(kind)


def setup_inputs(seed: int = 0, part: int = 0) -> dict:
    streams_of = jax.random.split(jax.random.key(seed), 15)
    own_keys = jax.random.split(jax.random.fold_in(streams_of[14], part), 15)
    x_new = scatter_about(own_keys[0], (STEPS, ROWS, DI), 1.0, 6.0, ((1, 4), (2, 4)))
    z_new = scatter_about(own_keys[1], (STEPS, ROWS, DI), 1.0, 6.0, ((1, 4), (2, 4)))
    ssm_state = scatter_about(own_keys[2], (ROWS, NS, DI), 0.5, 4.0, ((0, 4), (2, 4)))
    conv_state = scatter_about(own_keys[3], (ROWS, CONV_WIDTH - 1, DI), 1.0, 6.0, ((0, 4), (2, 4)))
    conv_weight = scatter_about(streams_of[4], (CONV_WIDTH, DI), 0.5, 3.0, ((1, 4),), jnp.float32)
    conv_bias = jnp.clip(jax.random.uniform(streams_of[5], (DI,), jnp.float32, -0.5, 0.5) * block_scale(streams_of[5], (DI,), ((0, 4),), -0.4, 0.0), -0.5, 0.5)
    proj_weight = draw_proj_weight(jax.random.fold_in(streams_of[14], 71), part)
    dt_weight = scatter_about(streams_of[7], (RANK, DI), RANK ** -0.5, 0.25, ((1, 4),))
    dt_bias = jnp.clip(-6.0 + 5.0 * jax.random.uniform(streams_of[8], (DI,), jnp.float32) ** block_scale(streams_of[8], (DI,), ((0, 4),), -0.2, 0.2), -6.0, -1.0)
    a_log = jnp.clip(2.77 * jax.random.uniform(streams_of[9], (NS, DI), jnp.float32) ** block_scale(streams_of[9], (NS, DI), ((1, 4),), -0.2, 0.2), 0.0, 2.77)
    skip_gain = jnp.clip(0.5 + 1.5 * jax.random.uniform(streams_of[10], (DI,), jnp.float32) ** block_scale(streams_of[10], (DI,), ((0, 4),), -0.2, 0.2), 0.5, 2.0)
    leave_slot = draw_leave_slot(jax.random.fold_in(jax.random.fold_in(streams_of[14], part), 71), part)
    dest_table = draw_dest_table(jax.random.fold_in(jax.random.fold_in(streams_of[14], part), 71), part)
    land_slot = draw_land_slot(jax.random.fold_in(jax.random.fold_in(streams_of[14], part), 71), part)
    return {"x_new": x_new, "z_new": z_new, "ssm_state": ssm_state, "conv_state": conv_state, "conv_weight": conv_weight, "conv_bias": conv_bias, "proj_weight": proj_weight, "dt_weight": dt_weight, "dt_bias": dt_bias, "a_log": a_log, "skip_gain": skip_gain, "leave_slot": leave_slot, "dest_table": dest_table, "land_slot": land_slot}


def migrate_rows(table, leave_slot, dest_table, land_slot):
    flat_dest = dest_table.reshape(-1)
    total_rows = flat_dest.shape[0]
    earlier = jnp.tril(flat_dest[:, None] == flat_dest[None, :], -1)
    arrival_rank = lax.optimization_barrier(jnp.sum(earlier.astype(jnp.int32), axis=1)).astype(jnp.int32)
    source_inst = jnp.arange(total_rows, dtype=jnp.int32) // MIG
    source_row = source_inst * SLOTS + leave_slot.reshape(-1)
    target_row = flat_dest * SLOTS + land_slot[flat_dest, arrival_rank]
    return table.at[target_row].set(table[source_row])

def convolve(window, conv_weight, conv_bias):
    conv_sum = jnp.einsum('rjc,jc->rc', window.astype(jnp.float32), conv_weight.astype(jnp.float32)) + conv_bias
    return jax.nn.silu(conv_sum)

def reference(x_new, z_new, ssm_state, conv_state, conv_weight, conv_bias, proj_weight, dt_weight, dt_bias, a_log, skip_gain, leave_slot, dest_table, land_slot):
    moved_ssm = migrate_rows(ssm_state, leave_slot, dest_table, land_slot)
    moved_conv = migrate_rows(conv_state, leave_slot, dest_table, land_slot)
    hidden = moved_ssm.astype(jnp.float32)
    decay_rate = -jnp.exp(a_log)
    history = moved_conv
    results = []
    for step_index in range(STEPS):
        window = jnp.concatenate([history, x_new[step_index][:, None, :]], axis=1)
        conv_out = convolve(window, conv_weight, conv_bias)
        history = window[:, 1:, :]
        conv_bf16 = conv_out.astype(jnp.bfloat16)
        projected = jnp.dot(conv_bf16, proj_weight, preferred_element_type=jnp.float32)
        dt_raw = projected[:, :RANK]
        b_part = projected[:, RANK:RANK + NS]
        c_part = projected[:, RANK + NS:]
        normed = (dt_raw * lax.rsqrt(lax.optimization_barrier(jnp.mean(dt_raw * dt_raw, axis=1, keepdims=True)) + 1e-06)).astype(jnp.bfloat16)
        step_size = jax.nn.softplus(jnp.dot(normed, dt_weight, preferred_element_type=jnp.float32) + dt_bias)
        hidden = jnp.exp(step_size[:, None, :] * decay_rate[None, :, :]) * hidden + (step_size * conv_out)[:, None, :] * b_part[:, :, None]
        readout = lax.optimization_barrier(jnp.sum(c_part[:, :, None] * hidden, axis=1)) + skip_gain * conv_out
        results.append((readout * jax.nn.silu(z_new[step_index].astype(jnp.float32))).astype(jnp.bfloat16))
    return (jnp.stack(results), hidden.astype(jnp.bfloat16), history)
```

```python
import functools
import math

import jax
import jax.numpy as jnp
from jax import lax
from jax.experimental import pallas as pl
from jax.experimental.pallas import tpu as pltpu
from jax.sharding import PartitionSpec as P

F32 = jnp.float32
BF16 = jnp.bfloat16
LANES = 128
LOG2E = math.log2(math.e)
MIB = 1 << 20


def iota(shape, dim):
    return lax.broadcasted_iota(jnp.int32, shape, dim)


def silu(value):
    return value / (1.0 + jnp.exp(-value))


def gather_kernel(n, cap, chunks, leave, dest, land, own_ref, conv, ssm, *rest):
    peers = n - 1
    conv_send = rest[:peers]
    ssm_send = rest[peers : 2 * peers]
    land_tab, stay_tab, leave_tab, flags, sems = rest[2 * peers :]
    mig = leave.shape[1]
    slots = ssm.shape[0]
    taps = conv.shape[0]
    width = conv.shape[2] // chunks
    own = own_ref[0]

    def clear(i, _):
        leave_tab[i] = -1
        land_tab[i] = -1
        return 0

    lax.fori_loop(0, n * cap, clear, 0, unroll=True)

    for pos in range(mig):
        peer = dest[own, pos] ^ own
        rank = 0
        for earlier in range(pos):
            rank = rank + jnp.where(dest[own, earlier] ^ own == peer, 1, 0)
        leave_tab[peer * cap + rank] = leave[0, pos]

    def copy(k, s, slot):
        return pltpu.make_async_copy(ssm.at[slot], ssm_send[k - 1].at[s], sems.at[k - 1, s])

    for k in range(1, n):
        for s in range(cap):
            slot = leave_tab[k * cap + s]

            @pl.when(slot >= 0)
            def _():
                copy(k, s, slot).start()

    rows = chunks * taps * cap
    row = iota((rows, taps * slots), 0)
    col = iota((rows, taps * slots), 1)
    place = lax.rem(row, cap)
    tap = lax.rem(lax.div(row, cap), taps)
    chunk = lax.div(row, taps * cap)
    table = conv[...].reshape(taps * slots, conv.shape[2])
    picks = []
    for k in range(1, n):
        source = jnp.full(row.shape, -1, jnp.int32)
        for s in range(cap):
            slot = leave_tab[k * cap + s]
            source = jnp.where((place == s) & (slot >= 0), tap * slots + slot, source)
        picks.append(source == col)
    for k in range(1, n):
        total = jnp.zeros((rows, width), F32)
        for q in range(chunks):
            pick = jnp.where(picks[k - 1] & (chunk == q), 1.0, 0.0).astype(BF16)
            total += jnp.dot(pick, table[:, q * width : (q + 1) * width], preferred_element_type=F32)
        conv_send[k - 1][...] = total.astype(BF16)

    def arrivals(source, rank):
        def one(pos, carry):
            rank, place = carry
            hit = dest[source, pos] == own

            @pl.when(hit)
            def _():
                land_tab[(source ^ own) * cap + place] = land[0, rank]

            step = jnp.where(hit, 1, 0)
            return rank + step, place + step

        return lax.fori_loop(0, mig, one, (rank, 0))[0]

    lax.fori_loop(0, n, arrivals, 0)

    def unset(i, _):
        flags[i] = 0
        return 0

    lax.fori_loop(0, slots, unset, 0, unroll=8)
    for pos in range(mig):
        flags[leave[0, pos]] = 1

    def staying(slot, count):
        @pl.when(flags[slot] == 0)
        def _():
            stay_tab[count] = slot

        return count + 1 - flags[slot]

    lax.fori_loop(0, slots, staying, 0)

    for k in range(1, n):
        for s in range(cap):
            slot = leave_tab[k * cap + s]

            @pl.when(slot >= 0)
            def _():
                copy(k, s, slot).wait()


def project_kernel(n, cap, land_tab, *rest):
    peers = n - 1
    got = rest[:peers]
    conv, x_new, weight, bias, proj = rest[peers : peers + 5]
    conv_out, new_conv, own_sum, send_sum, total = rest[peers + 5 :]
    q = pl.program_id(0)
    taps, slots, width = conv.shape
    rows = got[0].shape[0]
    cols = proj.shape[0]

    col = iota((1, peers * rows), 1)
    inner = lax.rem(col, rows)
    target = jnp.full(col.shape, -1, jnp.int32)
    slot_row = iota((slots, 1), 0)
    arrived = jnp.zeros((slots, 1), jnp.bool_)
    for k in range(1, n):
        for s in range(cap):
            slot = land_tab[k * cap + s]
            target = jnp.where((lax.div(col, rows) == k - 1) & (lax.rem(inner, cap) == s), slot, target)
            arrived = arrived | (slot_row == slot)
    tap = lax.rem(lax.div(inner, cap), taps)
    target = jnp.where(lax.div(inner, taps * cap) == q, target, -1)
    grid_row = iota((slots, peers * rows), 0)
    incoming = jnp.concatenate([g[...] for g in got], axis=0)
    history = []
    for j in range(taps):
        pick = jnp.where(grid_row == jnp.where(tap == j, target, -1), 1.0, 0.0).astype(BF16)
        moved = jnp.dot(pick, incoming, preferred_element_type=F32)
        history.append(jnp.where(arrived, moved, conv[j].astype(F32)))
    new_conv[0] = history[taps - 1].astype(BF16)
    new_conv[1] = x_new[0]
    new_conv[2] = x_new[1]
    window = history + [x_new[0].astype(F32), x_new[1].astype(F32)]
    halves = []
    for t in range(2):
        value = window[t] * weight[0:1, :]
        for j in range(1, taps + 1):
            value += window[t + j] * weight[j : j + 1, :]
        value = silu(value + bias[...])
        conv_out[t] = value
        halves.append(value.astype(BF16))
    part = lax.dot_general(
        jnp.concatenate(halves, axis=0), proj[...], (((1,), (1,)), ((), ())), preferred_element_type=F32
    )

    @pl.when(q == 0)
    def _():
        total[...] = jnp.zeros_like(total)

    total[:, :cols] += part

    @pl.when(q == pl.num_programs(0) - 1)
    def _():
        rank = total.shape[1] - LANES
        own_sum[...] = total[...]
        send_sum[:, :rank] = total[:, :rank].astype(BF16)
        tail = total[:, rank:]
        high = tail.astype(BF16).astype(F32)
        send_sum[:, rank:] = (high + pltpu.roll(tail - high, cols - rank, 1)).astype(BF16)


def spread(values, lane, states):
    rows = values.shape[0]
    wide = jnp.broadcast_to(values[:, None, :], (rows, states, LANES))
    keep = iota(wide.shape, 2) == iota(wide.shape, 1) + lane
    wide = jnp.where(keep, wide, 0.0).reshape(rows * states, LANES)
    high = wide.astype(BF16)
    low = (wide - high.astype(F32)).astype(BF16)
    ones = jnp.ones((LANES, LANES), BF16)
    both = jnp.dot(high, ones, preferred_element_type=F32) + jnp.dot(low, ones, preferred_element_type=F32)
    return both.reshape(rows, states, LANES)


def advance(hidden, rate, steps):
    sums = []
    for size, drive, b_part, c_part in steps:
        hidden = jnp.exp2(size * rate) * hidden + drive * b_part
        sums.append(jnp.sum(c_part * hidden, axis=0, keepdims=True))
    return hidden, sums


def wide(tile, lanes):
    return jnp.concatenate([tile] * (lanes // LANES), axis=1)


def stay_kernel(n, tps, cap, stays, land_tab, stay_tab, own_sum, *rest):
    got = rest[: tps - 1]
    dt_weight, dt_bias, a_log, skip, conv_out, z_new, ssm = rest[tps - 1 : tps + 6]
    new_ssm, out, size_m, drive_m, skip_m, gate_m, b_m, c_m = rest[tps + 6 : tps + 14]
    normed, b_all, c_all, size_s, drive_s, skip_s, gate_s, read_s = rest[tps + 14 :]
    rank = dt_weight.shape[0]
    states, width = a_log.shape
    slots = ssm.shape[0]
    movers = (n - 1) * cap

    @pl.when(pl.program_id(0) == 0)
    def _():
        raw = own_sum[:, :rank]
        tail = own_sum[:, rank:]
        for g in got:
            raw += g[:, :rank].astype(F32)
            piece = g[:, rank:].astype(F32)
            tail += piece + pltpu.roll(piece, LANES - 2 * states, 1)
        scale = lax.rsqrt(jnp.mean(raw * raw, axis=1, keepdims=True) + 1e-06)
        normed[...] = (raw * scale).astype(BF16)
        b_all[...] = spread(tail, 0, states)
        c_all[...] = spread(tail, states, states)
        for t in range(2):
            for k in range(1, n):
                for s in range(cap):
                    slot = jnp.maximum(land_tab[k * cap + s], 0)
                    at = t * movers + (k - 1) * cap + s
                    b_m[at] = b_all[t * slots + slot]
                    c_m[at] = c_all[t * slots + slot]

    pre = jnp.dot(normed[...], dt_weight[...], preferred_element_type=F32) + dt_bias[...]
    size = jnp.maximum(pre, 0.0) + jnp.log1p(jnp.exp(-jnp.abs(pre)))
    conv = conv_out[...].reshape(2 * slots, width)
    gate = silu(z_new[...].reshape(2 * slots, width).astype(F32))
    size_s[...] = size
    drive_s[...] = size * conv
    skip_s[...] = skip[...] * conv
    gate_s[...] = gate
    rate = -LOG2E * jnp.exp(a_log[...])

    def one(i, _):
        slot = stay_tab[i]
        steps = []
        for t in range(2):
            at = t * slots + slot
            steps.append(
                (
                    size_s[pl.ds(at, 1), :],
                    drive_s[pl.ds(at, 1), :],
                    wide(b_all[at], width),
                    wide(c_all[at], width),
                )
            )
        hidden, sums = advance(ssm[slot].astype(F32), rate, steps)
        new_ssm[slot] = hidden.astype(BF16)
        for t in range(2):
            read_s[pl.ds(t * slots + slot, 1), :] = sums[t]
        return 0

    lax.fori_loop(0, stays, one, 0)
    done = (read_s[...] + skip_s[...]) * gate_s[...]
    out[...] = done.reshape(2, slots, width).astype(BF16)
    for t in range(2):
        for k in range(1, n):
            for s in range(cap):
                from_row = pl.ds(t * slots + jnp.maximum(land_tab[k * cap + s], 0), 1)
                at = t * movers + (k - 1) * cap + s
                for ref, source in ((size_m, size_s), (drive_m, drive_s), (skip_m, skip_s), (gate_m, gate_s)):
                    ref[at : at + 1, :] = source[from_row, :]


def arrive_kernel(n, cap, land_tab, *rest):
    peers = n - 1
    got = rest[:peers]
    a_log, size_m, drive_m, skip_m, gate_m, b_m, c_m, out_in, _ = rest[peers : peers + 9]
    out, new_ssm, fresh, read_s, sems = rest[peers + 9 :]
    step = pl.program_id(0)
    states, width = a_log.shape
    movers = peers * cap
    slots = out.shape[1]
    rate = -LOG2E * jnp.exp(a_log[...])

    def copy(i, place):
        lanes = pl.ds(pl.multiple_of(place * width, width), width)
        return pltpu.make_async_copy(
            fresh.at[place, i], new_ssm.at[land_tab[cap + i], :, lanes], sems.at[place, i]
        )

    read_s[...] = jnp.zeros_like(read_s)
    for k in range(1, n):
        for s in range(cap):
            i = (k - 1) * cap + s
            steps = []
            for t in range(2):
                at = t * movers + i
                steps.append(
                    (
                        size_m[at : at + 1, :],
                        drive_m[at : at + 1, :],
                        wide(b_m[at], width),
                        wide(c_m[at], width),
                    )
                )
            hidden, sums = advance(got[k - 1][s].astype(F32), rate, steps)
            fresh[step, i] = hidden.astype(BF16)

            @pl.when(land_tab[cap + i] >= 0)
            def _():
                copy(i, step).start()

            for t in range(2):
                at = t * movers + i
                done = (sums[t] + skip_m[at : at + 1, :]) * gate_m[at : at + 1, :]
                read_s[t, i : i + 1, :] = done
    pad = read_s.shape[1]
    row = iota((slots, pad), 0)
    col = iota((1, pad), 1)
    target = jnp.full(col.shape, -1, jnp.int32)
    arrived = jnp.zeros((slots, 1), jnp.bool_)
    slot_row = iota((slots, 1), 0)
    for i in range(movers):
        slot = land_tab[cap + i]
        target = jnp.where(col == i, slot, target)
        arrived = arrived | (slot_row == slot)
    pick = jnp.where(row == target, 1.0, 0.0).astype(BF16)
    for t in range(2):
        placed = jnp.dot(pick, read_s[t].astype(BF16), preferred_element_type=F32)
        out[t] = jnp.where(arrived, placed, out_in[t].astype(F32)).astype(BF16)

    @pl.when(step == pl.num_programs(0) - 1)
    def _():
        for place in range(fresh.shape[0]):
            for i in range(movers):

                @pl.when(land_tab[cap + i] >= 0)
                def _():
                    copy(i, place).wait()


def exchange(value, axis, k, n):
    return lax.ppermute(value, axis, [(i, i ^ k) for i in range(n)])


def spec(shape, index=None):
    if index is None:
        return pl.BlockSpec(shape, lambda i: (0,) * len(shape))
    return pl.BlockSpec(shape, index)


def last(*lead):
    return pl.BlockSpec(lead, lambda i: (0,) * (len(lead) - 1) + (i,))


def params(mib):
    return pltpu.CompilerParams(vmem_limit_bytes=mib * MIB)


def local(
    n,
    tps,
    x_new,
    z_new,
    ssm_state,
    conv_state,
    conv_weight,
    conv_bias,
    proj_weight,
    dt_weight,
    dt_bias,
    a_log,
    skip_gain,
    leave_slot,
    dest_table,
    land_slot,
):
    slots, states, channels = ssm_state.shape
    mig = leave_slot.shape[1]
    taps = conv_state.shape[1]
    rank = dt_weight.shape[0]
    peers = n - 1
    cap = max(2, (mig + n - 2) // (n - 1))
    movers = peers * cap
    stays = slots - mig
    chunks = 16 // math.gcd(16, taps * cap)
    rows = chunks * taps * cap
    width = channels // chunks
    smem = pl.BlockSpec(memory_space=pltpu.SMEM)
    vmem = pl.BlockSpec(memory_space=pltpu.VMEM)
    hbm = pl.BlockSpec(memory_space=pl.ANY)
    shape = jax.ShapeDtypeStruct
    own = lax.axis_index("inst").astype(jnp.int32).reshape(1)
    conv_t = jnp.transpose(conv_state, (1, 0, 2))
    proj_t = proj_weight.T
    cols = proj_t.shape[0]
    padded = rank + LANES
    bias_row = conv_bias.reshape(1, channels)
    dt_bias_row = dt_bias.reshape(1, channels)
    skip_row = skip_gain.reshape(1, channels)

    with jax.named_scope("gather_leaving"):
        sent = pl.pallas_call(
            functools.partial(gather_kernel, n, cap, chunks),
            out_shape=[shape((rows, width), BF16)] * peers
            + [shape((cap, states, channels), BF16)] * peers
            + [shape((n * cap,), jnp.int32), shape((slots,), jnp.int32)],
            in_specs=[smem] * 4 + [vmem, hbm],
            out_specs=[vmem] * peers + [hbm] * peers + [smem, smem],
            scratch_shapes=[
                pltpu.SMEM((n * cap,), jnp.int32),
                pltpu.SMEM((slots,), jnp.int32),
                pltpu.SemaphoreType.DMA((peers, cap)),
            ],
            compiler_params=params(24),
        )(leave_slot, dest_table, land_slot, own, conv_t, ssm_state)
    conv_sent, ssm_sent = sent[:peers], sent[peers : 2 * peers]
    land_tab, stay_tab = sent[2 * peers :]

    order = sorted(range(1, n), key=lambda k: -k)
    conv_got, ssm_got = {}, {}
    for k in order:
        conv_got[k] = exchange(conv_sent[k - 1], "inst", k, n)
    for k in order:
        ssm_got[k] = exchange(ssm_sent[k - 1], "inst", k, n)

    with jax.named_scope("project"):
        conv_out, new_conv, own_sum, send_sum = pl.pallas_call(
            functools.partial(project_kernel, n, cap),
            grid=(chunks,),
            out_shape=[
                shape((2, slots, channels), F32),
                shape((taps, slots, channels), BF16),
                shape((2 * slots, padded), F32),
                shape((2 * slots, padded), BF16),
            ],
            in_specs=[smem]
            + [spec((rows, width))] * peers
            + [
                last(taps, slots, width),
                last(2, slots, width),
                last(taps + 1, width),
                last(1, width),
                last(cols, width),
            ],
            out_specs=[
                last(2, slots, width),
                last(taps, slots, width),
                spec((2 * slots, padded)),
                spec((2 * slots, padded)),
            ],
            scratch_shapes=[pltpu.VMEM((2 * slots, padded), F32)],
            compiler_params=params(32),
        )(
            land_tab,
            *[conv_got[k] for k in range(1, n)],
            conv_t,
            x_new,
            conv_weight,
            bias_row,
            proj_t,
        )

    sums_got = [exchange(send_sum, "tp", k, tps) for k in range(tps - 1, 0, -1)]

    step = min(512, channels)
    with jax.named_scope("update_staying"):
        stay_out = pl.pallas_call(
            functools.partial(stay_kernel, n, tps, cap, stays),
            grid=(channels // step,),
            out_shape=[
                shape((slots, states, channels), BF16),
                shape((2, slots, channels), BF16),
                shape((2 * movers, channels), F32),
                shape((2 * movers, channels), F32),
                shape((2 * movers, channels), F32),
                shape((2 * movers, channels), F32),
                shape((2 * movers, states, LANES), F32),
                shape((2 * movers, states, LANES), F32),
            ],
            in_specs=[smem, smem]
            + [spec((2 * slots, padded))] * tps
            + [
                last(rank, step),
                last(1, step),
                last(states, step),
                last(1, step),
                last(2, slots, step),
                last(2, slots, step),
                last(slots, states, step),
            ],
            out_specs=[last(slots, states, step), last(2, slots, step)]
            + [last(2 * movers, step)] * 4
            + [spec((2 * movers, states, LANES))] * 2,
            scratch_shapes=[
                pltpu.VMEM((2 * slots, rank), BF16),
                pltpu.VMEM((2 * slots, states, LANES), F32),
                pltpu.VMEM((2 * slots, states, LANES), F32),
            ]
            + [pltpu.VMEM((2 * slots, step), F32)] * 5,
            compiler_params=params(32),
        )(
            land_tab,
            stay_tab,
            own_sum,
            *sums_got,
            dt_weight,
            dt_bias_row,
            a_log,
            skip_row,
            conv_out,
            z_new,
            ssm_state,
        )
    new_ssm, out_stay, *moving = stay_out

    wide_step = min(1024, channels)
    grid = channels // wide_step
    pad = -(-movers // 16) * 16
    with jax.named_scope("update_arrived"):
        outputs, new_ssm = pl.pallas_call(
            functools.partial(arrive_kernel, n, cap),
            grid=(grid,),
            out_shape=[shape((2, slots, channels), BF16), shape((slots, states, channels), BF16)],
            in_specs=[smem]
            + [last(cap, states, wide_step)] * peers
            + [last(states, wide_step)]
            + [last(2 * movers, wide_step)] * 4
            + [spec((2 * movers, states, LANES))] * 2
            + [last(2, slots, wide_step), hbm],
            out_specs=[last(2, slots, wide_step), hbm],
            scratch_shapes=[
                pltpu.VMEM((grid, movers, states, wide_step), BF16),
                pltpu.VMEM((2, pad, wide_step), F32),
                pltpu.SemaphoreType.DMA((grid, movers)),
            ],
            input_output_aliases={1 + peers + 8: 1},
            compiler_params=params(32),
        )(land_tab, *[ssm_got[k] for k in range(1, n)], a_log, *moving, out_stay, new_ssm)
    return outputs, new_ssm, jnp.transpose(new_conv, (1, 0, 2))


def solution(mesh):
    return jax.shard_map(
        functools.partial(local, mesh.shape["inst"], mesh.shape["tp"]),
        mesh=mesh,
        in_specs=(
            P(None, ("groups", "inst"), "tp"),
            P(None, ("groups", "inst"), "tp"),
            P(("groups", "inst"), None, "tp"),
            P(("groups", "inst"), None, "tp"),
            P(None, "tp"),
            P("tp"),
            P("tp", None),
            P(None, "tp"),
            P("tp"),
            P(None, "tp"),
            P("tp"),
            P(("groups", "inst"), None),
            P("groups", None),
            P(("groups", "inst"), None),
        ),
        out_specs=(
            P(None, ("groups", "inst"), "tp"),
            P(("groups", "inst"), None, "tp"),
            P(("groups", "inst"), None, "tp"),
        ),
        check_vma=False,
    )
```

```python
import functools
import math

import jax
import jax.numpy as jnp
from jax import lax
from jax.experimental import pallas as pl
from jax.experimental.pallas import tpu as pltpu
from jax.sharding import PartitionSpec as P

F32 = jnp.float32
BF16 = jnp.bfloat16
LANES = 128
LOG2E = math.log2(math.e)
MIB = 1 << 20


def iota(shape, dim):
    return lax.broadcasted_iota(jnp.int32, shape, dim)


def silu(value):
    return value / (1.0 + jnp.exp(-value))


def gather_conv_kernel(n, cap, chunks, own_ref, leave_hbm, dest_hbm, conv_hbm, ssm, *rest):
    peers = n - 1
    send = rest[:peers]
    near, leave_tab, leave, dest, conv, sems, row_sems = rest[peers:]
    mig = leave.shape[1]
    taps, slots, channels = conv.shape
    width = channels // chunks
    own = own_ref[0]
    tables = [
        pltpu.make_async_copy(leave_hbm, leave, sems.at[chunks]),
        pltpu.make_async_copy(dest_hbm, dest, sems.at[chunks + 1]),
    ]
    for table in tables:
        table.start()
    loads = []
    for q in range(chunks):
        lanes = pl.ds(q * width, width)
        loads.append(pltpu.make_async_copy(conv_hbm.at[:, :, lanes], conv.at[:, :, lanes], sems.at[q]))
        loads[q].start()
    for i in range(n * cap):
        leave_tab[i] = -1
    for table in tables:
        table.wait()
    away = [dest[own, pos] ^ own for pos in range(mig)]
    for pos in range(mig):
        place = 0
        for earlier in range(pos):
            place = place + jnp.where(away[earlier] == away[pos], 1, 0)
        leave_tab[away[pos] * cap + place] = leave[0, pos]
    pairs = row_copies(ssm, [near], row_sems, leave_tab, cap, [1])
    start_all(pairs)

    rows = chunks * taps * cap
    row = iota((peers * rows, 1), 0)
    inner = lax.rem(row, rows)
    place = lax.rem(inner, cap)
    tap = lax.rem(lax.div(inner, cap), taps)
    chunk = lax.div(inner, taps * cap)
    peer = lax.div(row, rows)
    source = jnp.full(row.shape, -1, jnp.int32)
    for k in range(1, n):
        for s in range(cap):
            slot = leave_tab[k * cap + s]
            source = jnp.where((peer == k - 1) & (place == s) & (slot >= 0), tap * slots + slot, source)
    pick = jnp.where(source == iota((peers * rows, taps * slots), 1), 1.0, 0.0)
    total = None
    for q in range(chunks):
        loads[q].wait()
        part = jnp.dot(
            jnp.where(chunk == q, pick, 0.0).astype(BF16),
            conv[:, :, q * width : (q + 1) * width].reshape(taps * slots, width),
            preferred_element_type=F32,
        )
        total = part if total is None else total + part
    for k in range(1, n):
        send[k - 1][...] = total[(k - 1) * rows : k * rows, :].astype(BF16)
    wait_all(pairs)


def row_copies(ssm, send, sems, tab, cap, peer_list):
    pairs = []
    for at, k in enumerate(peer_list):
        for s in range(cap):
            slot = tab[k * cap + s]
            pairs.append((slot >= 0, pltpu.make_async_copy(ssm.at[slot], send[at].at[s], sems.at[at, s])))
    return pairs


def start_all(pairs):
    for present, copy in pairs:
        pl.when(present)(copy.start)


def wait_all(pairs):
    for present, copy in pairs:
        pl.when(present)(copy.wait)


def gather_ssm_kernel(n, cap, peer_list, own_ref, leave_tab, leave_hbm, dest_hbm, land_hbm, ssm, _, *rest):
    send = rest[: len(peer_list)]
    land_tab, stay_tab, leave, dest, land, flags, sems, table_sems = rest[len(peer_list) :]
    mig = leave.shape[1]
    slots = ssm.shape[0]
    own = own_ref[0]
    tables = [
        pltpu.make_async_copy(source, target, table_sems.at[i])
        for i, (source, target) in enumerate(((leave_hbm, leave), (dest_hbm, dest), (land_hbm, land)))
    ]
    for table in tables:
        table.start()
    pairs = row_copies(ssm, send, sems, leave_tab, cap, peer_list)
    start_all(pairs)
    for i in range(n * cap + 1):
        land_tab[i] = -1
    for i in range(slots):
        flags[i] = 0
    for table in tables:
        table.wait()

    def arrivals(source, rank):
        base = (source ^ own) * cap
        place = 0
        for pos in range(mig):
            hit = jnp.where(dest[source, pos] == own, 1, 0)
            land_tab[jnp.where(hit == 1, base + place, n * cap)] = land[0, jnp.minimum(rank, mig - 1)]
            rank, place = rank + hit, place + hit
        return rank

    if n <= 4:
        rank = 0
        for source in range(n):
            rank = arrivals(source, rank)
    else:
        lax.fori_loop(0, n, arrivals, 0)
    for pos in range(mig):
        flags[leave[0, pos]] = 1
    count = 0
    for slot in range(slots):
        stay_tab[count] = slot
        count = count + 1 - flags[slot]
    wait_all(pairs)


def project_kernel(n, cap, chunks, land_tab, _, *rest):
    peers = n - 1
    got = rest[:peers]
    conv, x_new, weight, bias, proj = rest[peers : peers + 5]
    conv_out, new_conv, own_sum, send_sum, newest, sems = rest[peers + 5 :]
    taps, slots, channels = conv.shape
    width = channels // chunks
    rows = got[0].shape[0]
    cols = proj.shape[0]
    store = [pltpu.make_async_copy(x_new.at[t], new_conv.at[taps - 2 + t], sems.at[t]) for t in range(2)]
    store.append(pltpu.make_async_copy(newest, new_conv.at[0], sems.at[2]))
    store[0].start()
    store[1].start()

    col = iota((1, peers * rows), 1)
    inner = lax.rem(col, rows)
    target = jnp.full(col.shape, -1, jnp.int32)
    slot_row = iota((slots, 1), 0)
    arrived = jnp.zeros((slots, 1), jnp.bool_)
    for k in range(1, n):
        for s in range(cap):
            slot = land_tab[k * cap + s]
            target = jnp.where((lax.div(col, rows) == k - 1) & (lax.rem(inner, cap) == s), slot, target)
            arrived = arrived | (slot_row == slot)
    tap = lax.rem(lax.div(inner, cap), taps)
    chunk = lax.div(inner, taps * cap)
    grid_row = iota((slots, peers * rows), 0)
    incoming = jnp.concatenate([g[...] for g in got], axis=0)
    total = jnp.zeros((2 * slots, cols), F32)
    for q in range(chunks):
        lanes = slice(q * width, (q + 1) * width)
        history = []
        for j in range(taps):
            pick = grid_row == jnp.where((tap == j) & (chunk == q), target, -1)
            moved = jnp.dot(jnp.where(pick, 1.0, 0.0).astype(BF16), incoming, preferred_element_type=F32)
            history.append(jnp.where(arrived, moved, conv[j, :, lanes].astype(F32)))
        newest[:, lanes] = history[taps - 1].astype(BF16)
        window = history + [x_new[t, :, lanes].astype(F32) for t in range(2)]
        halves = []
        for t in range(2):
            value = window[t] * weight[0:1, lanes]
            for j in range(1, taps + 1):
                value += window[t + j] * weight[j : j + 1, lanes]
            value = silu(value + bias[:, lanes])
            conv_out[t * slots : (t + 1) * slots, lanes] = value
            halves.append(value.astype(BF16))
        total += lax.dot_general(
            jnp.concatenate(halves, axis=0),
            proj[:, lanes],
            (((1,), (1,)), ((), ())),
            preferred_element_type=F32,
        )
    store[2].start()
    padded = own_sum.shape[1]
    rank = padded - LANES
    own_sum[:, rank:] = jnp.zeros((2 * slots, LANES), F32)
    own_sum[:, :cols] = total
    tail = own_sum[:, rank:]
    send_sum[:, :rank] = total[:, :rank].astype(BF16)
    high = tail.astype(BF16).astype(F32)
    send_sum[:, rank:] = (high + pltpu.roll(tail - high, cols - rank, 1)).astype(BF16)
    for copy in store:
        copy.wait()


def spread(values, lane, states):
    rows = values.shape[0]
    wide = jnp.broadcast_to(values[:, None, :], (rows, states, LANES))
    keep = iota(wide.shape, 2) == iota(wide.shape, 1) + lane
    wide = jnp.where(keep, wide, 0.0).reshape(rows * states, LANES)
    high = wide.astype(BF16)
    low = (wide - high.astype(F32)).astype(BF16)
    ones = jnp.ones((LANES, LANES), BF16)
    both = jnp.dot(high, ones, preferred_element_type=F32) + jnp.dot(low, ones, preferred_element_type=F32)
    return both.reshape(rows, states, LANES)


def spread_diagonal(values, lane, states, rows):
    cols = rows * states
    pick = iota((LANES, cols), 0) == lax.rem(iota((LANES, cols), 1), states) + lane
    pick = jnp.where(pick, 1.0, 0.0).astype(BF16)
    keep = lax.div(iota((values.shape[0], cols), 1), states) == iota((values.shape[0], cols), 0)
    high = values.astype(BF16)
    low = (values - high.astype(F32)).astype(BF16)
    parts = [jnp.where(keep, jnp.dot(v, pick, preferred_element_type=F32), 0.0) for v in (high, low)]
    return jnp.concatenate(parts, axis=0).astype(BF16)


def read(weights, hidden):
    both = jnp.dot(weights, hidden.reshape(-1, hidden.shape[2]), preferred_element_type=F32)
    half = both.shape[0] // 2
    return both[:half] + both[half:]


def advance(hidden, rate, size, drive, b_part):
    return jnp.exp2(size * rate) * hidden + drive * b_part


def wide(tile, lanes):
    return jnp.concatenate([tile] * (lanes // LANES), axis=1)


def gate_kernel(n, cap, land_tab, conv_out, z_new, skip, a_log, ssm, dt_weight, *rest):
    ssm_held, weight_held, gate, skipped, rate, conv_m, skip_m, gate_m, sems = rest
    slots = conv_out.shape[0] // 2
    held = [
        pltpu.make_async_copy(ssm, ssm_held, sems.at[0]),
        pltpu.make_async_copy(dt_weight, weight_held, sems.at[1]),
    ]
    for copy in held:
        copy.start()
    gate[...] = silu(z_new[...].astype(F32))
    skipped[...] = skip[...] * conv_out[...]
    rate[...] = -LOG2E * jnp.exp(a_log[...])
    movers = (n - 1) * cap
    for t in range(2):
        for i in range(movers):
            from_row = pl.ds(t * slots + jnp.maximum(land_tab[cap + i], 0), 1)
            at = t * movers + i
            for ref, source in ((conv_m, conv_out), (skip_m, skipped), (gate_m, gate)):
                ref[at : at + 1, :] = source[from_row, :]
    for copy in held:
        copy.wait()


def stay_kernel(n, tps, cap, stays, step, land_tab, stay_tab, own_sum, *rest):
    got = rest[: tps - 1]
    dt_weight, dt_bias, rate_ref, conv_out, skipped, gate, conv_m, ssm = rest[tps - 1 : tps + 7]
    new_ssm, out, size_m, drive_m, b_m, c_m = rest[tps + 7 : tps + 13]
    b_all, c_all, size_s, drive_s, middle, fresh, sems = rest[tps + 13 :]
    rank = dt_weight.shape[0]
    states, channels = rate_ref.shape
    slots = ssm.shape[0]
    movers = (n - 1) * cap

    raw = own_sum[:, :rank]
    tail = own_sum[:, rank:]
    for g in got:
        raw += g[:, :rank].astype(F32)
        piece = g[:, rank:].astype(F32)
        tail += piece + pltpu.roll(piece, LANES - 2 * states, 1)
    scale = lax.rsqrt(jnp.mean(raw * raw, axis=1, keepdims=True) + 1e-06)
    normed = (raw * scale).astype(BF16)
    b_all[...] = spread(tail, 0, states)
    middle[...] = jnp.zeros_like(middle)
    pad = c_m.shape[1] // 2
    row = iota((pad, slots), 0)
    slot_of = jnp.full(row.shape, -1, jnp.int32)
    for i in range(movers):
        slot_of = jnp.where(row == i, land_tab[cap + i], slot_of)
    pick = jnp.where(slot_of == iota((pad, slots), 1), 1.0, 0.0)
    for t in range(2):
        mine = tail[t * slots : (t + 1) * slots]
        c_all[t] = spread_diagonal(mine, states, states, slots)
        moved = jnp.dot(pick, mine, preferred_element_type=F32, precision=lax.Precision.HIGHEST)
        c_m[t] = spread_diagonal(moved, states, states, movers)
        for i in range(movers):
            b_m[t * movers + i] = b_all[t * slots + jnp.maximum(land_tab[cap + i], 0)]

    def store(place, lanes):
        return pltpu.make_async_copy(fresh.at[place], new_ssm.at[:, :, lanes], sems.at[place])

    def chunk(place, _):
        lanes = pl.ds(pl.multiple_of(place * step, step), step)
        pre = jnp.dot(normed, dt_weight[:, lanes], preferred_element_type=F32) + dt_bias[:, lanes]
        size = jnp.maximum(pre, 0.0) + jnp.log1p(jnp.exp(-jnp.abs(pre)))
        size_s[...] = size
        drive_s[...] = size * conv_out[:, lanes]
        rate = rate_ref[:, lanes]

        for i in range(movers):
            fresh[place, jnp.maximum(land_tab[cap + i], 0)] = jnp.zeros((states, step), BF16)

        def one(i, _):
            slot = stay_tab[i]
            hidden = ssm[slot, :, lanes].astype(F32)
            for t, after in ((0, middle.at[slot]), (1, fresh.at[place, slot])):
                at = pl.ds(t * slots + slot, 1)
                hidden = advance(hidden, rate, size_s[at, :], drive_s[at, :], wide(b_all[t * slots + slot], step))
                after[...] = hidden.astype(BF16)
            return 0

        lax.fori_loop(0, stays, one, 0, unroll=4)
        store(place, lanes).start()
        for t, after in ((0, middle[...]), (1, fresh[place])):
            at = slice(t * slots, (t + 1) * slots)
            out[at, lanes] = ((read(c_all[t], after) + skipped[at, lanes]) * gate[at, lanes]).astype(BF16)
        for t in range(2):
            for i in range(movers):
                from_row = pl.ds(t * slots + jnp.maximum(land_tab[cap + i], 0), 1)
                at = t * movers + i
                here = size_s[from_row, :]
                size_m[at : at + 1, lanes] = here
                drive_m[at : at + 1, lanes] = here * conv_m[at : at + 1, lanes]
        return 0

    lax.fori_loop(0, channels // step, chunk, 0)
    for place in range(channels // step):
        store(place, pl.ds(place * step, step)).wait()


def arrive_kernel(n, cap, full, step, land_tab, *rest):
    peers = n - 1
    got = rest[:peers]
    rate_ref, size_m, drive_m, skip_m, gate_m, b_m, c_m, out_in, _ = rest[peers : peers + 9]
    out, new_ssm, middle, fresh, rows_s, done_s, sems, out_sems = rest[peers + 9 :]
    states, channels = rate_ref.shape
    movers = peers * cap
    slots = out.shape[1]
    pad = rows_s.shape[1]
    row = iota((slots, pad), 0)
    col = iota((1, pad), 1)
    target = jnp.full(col.shape, -1, jnp.int32)
    arrived = jnp.zeros((slots, 1), jnp.bool_)
    slot_row = iota((slots, 1), 0)
    for i in range(movers):
        slot = land_tab[cap + i]
        target = jnp.where(col == i, slot, target)
        arrived = arrived | (slot_row == slot)
    pick = jnp.where(row == target, 1.0, 0.0).astype(BF16)
    rows_s[...] = jnp.zeros_like(rows_s)

    def copy(i, lanes, place):
        return pltpu.make_async_copy(fresh.at[place, i], new_ssm.at[land_tab[cap + i], :, lanes], sems.at[place, i])

    def copy_out(lanes, place):
        return pltpu.make_async_copy(done_s.at[place], out.at[:, :, lanes], out_sems.at[place])

    def chunk(place, _):
        lanes = pl.ds(pl.multiple_of(place * step, step), step)
        rate = rate_ref[:, lanes]
        for i in range(movers):
            hidden = got[i // cap][i % cap, :, lanes].astype(F32)
            if movers != full:
                hidden = jnp.where(land_tab[cap + i] >= 0, hidden, 0.0)
            for t, after in ((0, middle.at[i]), (1, fresh.at[place, i])):
                at = slice(t * movers + i, t * movers + i + 1)
                hidden = advance(hidden, rate, size_m[at, lanes], drive_m[at, lanes], wide(b_m[t * movers + i], step))
                after[...] = hidden.astype(BF16)
        for i in range(movers):
            pl.when(land_tab[cap + i] >= 0)(copy(i, lanes, place).start)
        for t in range(2):
            after = middle[...] if t == 0 else fresh[place]
            at = slice(t * movers, (t + 1) * movers)
            rows_s[t, :movers, :] = (read(c_m[t], after)[:movers] + skip_m[at, lanes]) * gate_m[at, lanes]
            placed = jnp.dot(pick, rows_s[t].astype(BF16), preferred_element_type=F32)
            kept = out_in[t * slots : (t + 1) * slots, lanes].astype(F32)
            done_s[place, t] = jnp.where(arrived, placed, kept).astype(BF16)
        copy_out(lanes, place).start()
        return 0

    lax.fori_loop(0, channels // step, chunk, 0)
    for place in range(channels // step):
        lanes = pl.ds(place * step, step)
        copy_out(lanes, place).wait()
        for i in range(movers):
            pl.when(land_tab[cap + i] >= 0)(copy(i, lanes, place).wait)


def exchange(value, axis, k, n):
    return lax.ppermute(value, axis, [(i, i ^ k) for i in range(n)])


def cost(flops):
    return pl.CostEstimate(flops=flops, bytes_accessed=0, transcendentals=0)


def params(mib):
    return pltpu.CompilerParams(vmem_limit_bytes=mib * MIB)


def local(
    n,
    tps,
    x_new,
    z_new,
    ssm_state,
    conv_state,
    conv_weight,
    conv_bias,
    proj_weight,
    dt_weight,
    dt_bias,
    a_log,
    skip_gain,
    leave_slot,
    dest_table,
    land_slot,
):
    slots, states, channels = ssm_state.shape
    mig = leave_slot.shape[1]
    taps = conv_state.shape[1]
    rank = dt_weight.shape[0]
    peers = n - 1
    cap = max(2, (mig + n - 2) // (n - 1))
    movers = peers * cap
    stays = slots - mig
    chunks = 16 // math.gcd(16, taps * cap)
    rows = chunks * taps * cap
    width = channels // chunks
    smem = pl.BlockSpec(memory_space=pltpu.SMEM)
    vmem = pl.BlockSpec(memory_space=pltpu.VMEM)
    anywhere = pl.BlockSpec(memory_space=pl.ANY)
    hbm = pl.BlockSpec(memory_space=pltpu.HBM)
    shape = jax.ShapeDtypeStruct
    def far(value):
        return pltpu.with_memory_space_constraint(value, pltpu.HBM)

    own = lax.axis_index("inst").astype(jnp.int32).reshape(1)
    conv_t = jnp.transpose(conv_state, (1, 0, 2))
    proj_t = proj_weight.T
    cols = proj_t.shape[0]
    padded = rank + LANES
    bias_row = conv_bias.reshape(1, channels)
    dt_bias_row = dt_bias.reshape(1, channels)
    skip_row = skip_gain.reshape(1, channels)

    with jax.named_scope("gather_conv"):
        *conv_sent, near, leave_tab = pl.pallas_call(
            functools.partial(gather_conv_kernel, n, cap, chunks),
            out_shape=[shape((rows, width), BF16)] * peers
            + [shape((cap, states, channels), BF16), shape((n * cap,), jnp.int32)],
            in_specs=[smem] + [hbm] * 4,
            out_specs=[vmem] * (peers + 1) + [smem],
            scratch_shapes=[
                pltpu.SMEM(leave_slot.shape, jnp.int32),
                pltpu.SMEM(dest_table.shape, jnp.int32),
                pltpu.VMEM((taps, slots, channels), BF16),
                pltpu.SemaphoreType.DMA((chunks + 2,)),
                pltpu.SemaphoreType.DMA((1, cap)),
            ],
            compiler_params=params(16),
        )(own, far(leave_slot), far(dest_table), far(conv_t), far(ssm_state))

    order = sorted(range(1, n), key=lambda k: -k)
    conv_got, ssm_got = {}, {}
    for k in order:
        conv_got[k] = exchange(conv_sent[k - 1], "inst", k, n)
    ssm_got[1] = exchange(near, "inst", 1, n)

    far_peers = list(range(2, n))
    with jax.named_scope("gather_ssm"):
        *ssm_sent, land_tab, stay_tab = pl.pallas_call(
            functools.partial(gather_ssm_kernel, n, cap, far_peers),
            out_shape=[shape((cap, states, channels), BF16)] * len(far_peers)
            + [shape((n * cap + 1,), jnp.int32), shape((slots,), jnp.int32)],
            in_specs=[smem] * 2 + [hbm] * 4 + [anywhere],
            out_specs=[vmem] * len(far_peers) + [smem, smem],
            scratch_shapes=[
                pltpu.SMEM(leave_slot.shape, jnp.int32),
                pltpu.SMEM(dest_table.shape, jnp.int32),
                pltpu.SMEM(land_slot.shape, jnp.int32),
                pltpu.SMEM((slots,), jnp.int32),
                pltpu.SemaphoreType.DMA((len(far_peers), cap)),
                pltpu.SemaphoreType.DMA((3,)),
            ],
            compiler_params=params(16),
        )(own, leave_tab, far(leave_slot), far(dest_table), far(land_slot), far(ssm_state), conv_got[1])
    for k in reversed(far_peers):
        ssm_got[k] = exchange(ssm_sent[k - 2], "inst", k, n)

    both = 2 * slots
    with jax.named_scope("project"):
        conv_out, new_conv, own_sum, send_sum = pl.pallas_call(
            functools.partial(project_kernel, n, cap, chunks),
            out_shape=[
                shape((both, channels), F32),
                shape((taps, slots, channels), BF16),
                shape((both, padded), F32),
                shape((both, padded), BF16),
            ],
            in_specs=[smem, anywhere] + [vmem] * (peers + 5),
            out_specs=[vmem, hbm, vmem, vmem],
            scratch_shapes=[pltpu.VMEM((slots, channels), BF16), pltpu.SemaphoreType.DMA((3,))],
            compiler_params=params(20),
            cost_estimate=cost(10**12),
        )(
            land_tab,
            ssm_got[1],
            *[conv_got[k] for k in range(1, n)],
            conv_t,
            x_new,
            conv_weight,
            bias_row,
            proj_t,
        )

    sums_got = [exchange(send_sum, "tp", k, tps) for k in range(tps - 1, 0, -1)]

    with jax.named_scope("gate"):
        ssm_held, weight_held, gate, skipped, rate, conv_m, skip_m, gate_m = pl.pallas_call(
            functools.partial(gate_kernel, n, cap),
            out_shape=[
                shape((slots, states, channels), BF16),
                shape((rank, channels), BF16),
            ]
            + [shape((both, channels), F32)] * 2
            + [shape((states, channels), F32)]
            + [shape((2 * movers, channels), F32)] * 3,
            in_specs=[smem] + [vmem] * 4 + [hbm] * 2,
            out_specs=[vmem] * 8,
            scratch_shapes=[pltpu.SemaphoreType.DMA((2,))],
            compiler_params=params(20),
        )(
            land_tab,
            conv_out,
            z_new.reshape(both, channels),
            skip_row,
            a_log,
            far(ssm_state),
            far(dt_weight),
        )

    step = min(512, channels)
    pad = -(-movers // 16) * 16
    with jax.named_scope("update_staying"):
        new_ssm, out_stay, size_m, drive_m, b_m, c_m = pl.pallas_call(
            functools.partial(stay_kernel, n, tps, cap, stays, step),
            out_shape=[
                shape((slots, states, channels), BF16),
                shape((both, channels), BF16),
                shape((2 * movers, channels), F32),
                shape((2 * movers, channels), F32),
                shape((2 * movers, states, LANES), F32),
                shape((2, 2 * pad, movers * states), BF16),
            ],
            in_specs=[smem, smem] + [vmem] * (tps + 8),
            out_specs=[hbm] + [vmem] * 5,
            scratch_shapes=[
                pltpu.VMEM((both, states, LANES), F32),
                pltpu.VMEM((2, both, slots * states), BF16),
                pltpu.VMEM((both, step), F32),
                pltpu.VMEM((both, step), F32),
                pltpu.VMEM((slots, states, step), BF16),
                pltpu.VMEM((channels // step, slots, states, step), BF16),
                pltpu.SemaphoreType.DMA((channels // step,)),
            ],
            compiler_params=params(24),
        )(
            land_tab,
            stay_tab,
            own_sum,
            *sums_got,
            weight_held,
            dt_bias_row,
            rate,
            conv_out,
            skipped,
            gate,
            conv_m,
            ssm_held,
        )

    parts = channels // step
    with jax.named_scope("update_arrived"):
        outputs, new_ssm = pl.pallas_call(
            functools.partial(arrive_kernel, n, cap, mig, step),
            out_shape=[shape((2, slots, channels), BF16), shape((slots, states, channels), BF16)],
            in_specs=[smem] + [vmem] * (peers + 8) + [hbm],
            out_specs=[hbm, hbm],
            scratch_shapes=[
                pltpu.VMEM((movers, states, step), BF16),
                pltpu.VMEM((parts, movers, states, step), BF16),
                pltpu.VMEM((2, pad, step), F32),
                pltpu.VMEM((parts, 2, slots, step), BF16),
                pltpu.SemaphoreType.DMA((parts, movers)),
                pltpu.SemaphoreType.DMA((parts,)),
            ],
            input_output_aliases={1 + peers + 8: 1},
            compiler_params=params(20),
        )(
            land_tab,
            *[ssm_got[k] for k in range(1, n)],
            rate,
            size_m,
            drive_m,
            skip_m,
            gate_m,
            b_m,
            c_m,
            out_stay,
            new_ssm,
        )
    return outputs, new_ssm, jnp.transpose(new_conv, (1, 0, 2))


def solution(mesh):
    return jax.shard_map(
        functools.partial(local, mesh.shape["inst"], mesh.shape["tp"]),
        mesh=mesh,
        in_specs=(
            P(None, ("groups", "inst"), "tp"),
            P(None, ("groups", "inst"), "tp"),
            P(("groups", "inst"), None, "tp"),
            P(("groups", "inst"), None, "tp"),
            P(None, "tp"),
            P("tp"),
            P("tp", None),
            P(None, "tp"),
            P("tp"),
            P(None, "tp"),
            P("tp"),
            P(("groups", "inst"), None),
            P("groups", None),
            P(("groups", "inst"), None),
        ),
        out_specs=(
            P(None, ("groups", "inst"), "tp"),
            P(("groups", "inst"), None, "tp"),
            P(("groups", "inst"), None, "tp"),
        ),
        check_vma=False,
    )
```

```python
import functools
import math

import jax
import jax.numpy as jnp
from jax import lax
from jax.experimental import pallas as pl
from jax.experimental.pallas import tpu as pltpu
from jax.sharding import PartitionSpec as P

F32 = jnp.float32
BF16 = jnp.bfloat16
LANES = 128
LOG2E = math.log2(math.e)
MIB = 1 << 20
PIECE = 512


def iota(shape, dim):
    return lax.broadcasted_iota(jnp.int32, shape, dim)


def silu(value):
    return value / (1.0 + jnp.exp(-value))


def gather_conv_kernel(n, cap, chunks, own_ref, leave_hbm, dest_hbm, conv_hbm, ssm, *rest):
    peers = n - 1
    send = rest[:peers]
    near, leave_tab, leave, dest, conv, sems, row_sems = rest[peers:]
    mig = leave.shape[1]
    taps, slots, channels = conv.shape
    width = channels // chunks
    own = own_ref[0]
    tables = [
        pltpu.make_async_copy(leave_hbm, leave, sems.at[chunks]),
        pltpu.make_async_copy(dest_hbm, dest, sems.at[chunks + 1]),
    ]
    for table in tables:
        table.start()
    loads = []
    for q in range(chunks):
        lanes = pl.ds(q * width, width)
        loads.append(pltpu.make_async_copy(conv_hbm.at[:, :, lanes], conv.at[:, :, lanes], sems.at[q]))
        loads[q].start()
    for i in range(n * cap):
        leave_tab[i] = -1
    for table in tables:
        table.wait()
    away = [dest[own, pos] ^ own for pos in range(mig)]
    for pos in range(mig):
        place = 0
        for earlier in range(pos):
            place = place + jnp.where(away[earlier] == away[pos], 1, 0)
        leave_tab[away[pos] * cap + place] = leave[0, pos]
    pairs = row_copies(ssm, [near], row_sems, leave_tab, cap, [1])
    start_all(pairs)

    rows = chunks * taps * cap
    row = iota((peers * rows, 1), 0)
    inner = lax.rem(row, rows)
    place = lax.rem(inner, cap)
    tap = lax.rem(lax.div(inner, cap), taps)
    chunk = lax.div(inner, taps * cap)
    peer = lax.div(row, rows)
    source = jnp.full(row.shape, -1, jnp.int32)
    for k in range(1, n):
        for s in range(cap):
            slot = leave_tab[k * cap + s]
            source = jnp.where((peer == k - 1) & (place == s) & (slot >= 0), tap * slots + slot, source)
    pick = jnp.where(source == iota((peers * rows, taps * slots), 1), 1.0, 0.0)
    total = None
    for q in range(chunks):
        loads[q].wait()
        part = jnp.dot(
            jnp.where(chunk == q, pick, 0.0).astype(BF16),
            conv[:, :, q * width : (q + 1) * width].reshape(taps * slots, width),
            preferred_element_type=F32,
        )
        total = part if total is None else total + part
    for k in range(1, n):
        send[k - 1][...] = total[(k - 1) * rows : k * rows, :].astype(BF16)
    wait_all(pairs)


def row_copies(ssm, send, sems, tab, cap, peer_list):
    pairs = []
    for at, k in enumerate(peer_list):
        for s in range(cap):
            slot = tab[k * cap + s]
            pairs.append((slot >= 0, pltpu.make_async_copy(ssm.at[slot], send[at].at[s], sems.at[at, s])))
    return pairs


def start_all(pairs):
    for present, copy in pairs:
        pl.when(present)(copy.start)


def wait_all(pairs):
    for present, copy in pairs:
        pl.when(present)(copy.wait)


def gather_ssm_kernel(n, cap, peer_list, own_ref, leave_tab, leave_hbm, dest_hbm, land_hbm, ssm, _, *rest):
    send = rest[: len(peer_list)]
    land_tab, stay_tab, leave, dest, land, flags, sems, table_sems = rest[len(peer_list) :]
    mig = leave.shape[1]
    slots = ssm.shape[0]
    own = own_ref[0]
    tables = [
        pltpu.make_async_copy(source, target, table_sems.at[i])
        for i, (source, target) in enumerate(((leave_hbm, leave), (dest_hbm, dest), (land_hbm, land)))
    ]
    for table in tables:
        table.start()
    pairs = row_copies(ssm, send, sems, leave_tab, cap, peer_list)
    start_all(pairs)
    for i in range(n * cap + 1):
        land_tab[i] = -1
    for i in range(slots):
        flags[i] = 0
    for table in tables:
        table.wait()

    def arrivals(source, rank):
        base = (source ^ own) * cap
        place = 0
        for pos in range(mig):
            hit = jnp.where(dest[source, pos] == own, 1, 0)
            land_tab[jnp.where(hit == 1, base + place, n * cap)] = land[0, jnp.minimum(rank, mig - 1)]
            rank, place = rank + hit, place + hit
        return rank

    if n <= 4:
        rank = 0
        for source in range(n):
            rank = arrivals(source, rank)
    else:
        lax.fori_loop(0, n, arrivals, 0)
    for pos in range(mig):
        flags[leave[0, pos]] = 1
    count = 0
    for slot in range(slots):
        stay_tab[count] = slot
        count = count + 1 - flags[slot]
    wait_all(pairs)


def project_kernel(n, cap, chunks, land_tab, _, *rest):
    peers = n - 1
    got = rest[:peers]
    conv, x_new, weight, bias, proj = rest[peers : peers + 5]
    conv_out, new_conv, own_sum, send_sum, newest, sems = rest[peers + 5 :]
    taps, slots, channels = conv.shape
    width = channels // chunks
    rows = got[0].shape[0]
    cols = proj.shape[0]
    store = [pltpu.make_async_copy(x_new.at[t], new_conv.at[taps - 2 + t], sems.at[t]) for t in range(2)]
    store.append(pltpu.make_async_copy(newest, new_conv.at[0], sems.at[2]))
    store[0].start()
    store[1].start()

    col = iota((1, peers * rows), 1)
    inner = lax.rem(col, rows)
    target = jnp.full(col.shape, -1, jnp.int32)
    slot_row = iota((slots, 1), 0)
    arrived = jnp.zeros((slots, 1), jnp.bool_)
    for k in range(1, n):
        for s in range(cap):
            slot = land_tab[k * cap + s]
            target = jnp.where((lax.div(col, rows) == k - 1) & (lax.rem(inner, cap) == s), slot, target)
            arrived = arrived | (slot_row == slot)
    tap = lax.rem(lax.div(inner, cap), taps)
    chunk = lax.div(inner, taps * cap)
    grid_row = iota((slots, peers * rows), 0)
    incoming = jnp.concatenate([g[...] for g in got], axis=0)
    total = jnp.zeros((2 * slots, cols), F32)
    for q in range(chunks):
        lanes = slice(q * width, (q + 1) * width)
        history = []
        for j in range(taps):
            pick = grid_row == jnp.where((tap == j) & (chunk == q), target, -1)
            moved = jnp.dot(jnp.where(pick, 1.0, 0.0).astype(BF16), incoming, preferred_element_type=F32)
            history.append(jnp.where(arrived, moved, conv[j, :, lanes].astype(F32)))
        newest[:, lanes] = history[taps - 1].astype(BF16)
        window = history + [x_new[t, :, lanes].astype(F32) for t in range(2)]
        halves = []
        for t in range(2):
            value = window[t] * weight[0:1, lanes]
            for j in range(1, taps + 1):
                value += window[t + j] * weight[j : j + 1, lanes]
            value = silu(value + bias[:, lanes])
            conv_out[t * slots : (t + 1) * slots, lanes] = value
            halves.append(value.astype(BF16))
        total += lax.dot_general(
            jnp.concatenate(halves, axis=0),
            proj[:, lanes],
            (((1,), (1,)), ((), ())),
            preferred_element_type=F32,
        )
    store[2].start()
    padded = own_sum.shape[1]
    rank = padded - LANES
    own_sum[:, rank:] = jnp.zeros((2 * slots, LANES), F32)
    own_sum[:, :cols] = total
    tail = own_sum[:, rank:]
    send_sum[:, :rank] = total[:, :rank].astype(BF16)
    high = tail.astype(BF16).astype(F32)
    send_sum[:, rank:] = (high + pltpu.roll(tail - high, cols - rank, 1)).astype(BF16)
    for copy in store:
        copy.wait()


def spread(values, lane, states):
    rows = values.shape[0]
    wide = jnp.broadcast_to(values[:, None, :], (rows, states, LANES))
    keep = iota(wide.shape, 2) == iota(wide.shape, 1) + lane
    wide = jnp.where(keep, wide, 0.0).reshape(rows * states, LANES)
    high = wide.astype(BF16)
    low = (wide - high.astype(F32)).astype(BF16)
    ones = jnp.ones((LANES, LANES), BF16)
    both = jnp.dot(high, ones, preferred_element_type=F32) + jnp.dot(low, ones, preferred_element_type=F32)
    return both.reshape(rows, states, LANES)


def spread_diagonal(values, lane, states, owner):
    cols = owner.shape[1]
    pick = iota((LANES, cols), 0) == lax.rem(iota((LANES, cols), 1), states) + lane
    pick = jnp.where(pick, 1.0, 0.0).astype(BF16)
    keep = owner == iota((values.shape[0], cols), 0)
    high = values.astype(BF16)
    low = (values - high.astype(F32)).astype(BF16)
    parts = [jnp.where(keep, jnp.dot(v, pick, preferred_element_type=F32), 0.0) for v in (high, low)]
    return jnp.concatenate(parts, axis=0).astype(BF16)


def read(weights, hidden):
    both = jnp.dot(weights, hidden.reshape(-1, hidden.shape[2]), preferred_element_type=F32)
    half = both.shape[0] // 2
    return both[:half] + both[half:]


def advance(hidden, rate, size, drive, b_part):
    return jnp.exp2(size * rate) * hidden + drive * b_part


def wide(tile, lanes):
    return jnp.concatenate([tile] * (lanes // LANES), axis=1)


def gate_kernel(conv_out, z_new, skip, a_log, ssm, dt_weight, ssm_held, weight_held, gate, skipped, rate, sems):
    held = [
        pltpu.make_async_copy(ssm, ssm_held, sems.at[0]),
        pltpu.make_async_copy(dt_weight, weight_held, sems.at[1]),
    ]
    for copy in held:
        copy.start()
    gate[...] = silu(z_new[...].astype(F32))
    skipped[...] = skip[...] * conv_out[...]
    rate[...] = -LOG2E * jnp.exp(a_log[...])
    for copy in held:
        copy.wait()


def both_steps(slot, slots, before, place, rate_ref, size, drive, b_all, middle, fresh):
    b_rows = [b_all[t * slots + slot] for t in range(2)]
    for start in range(0, rate_ref.shape[1], PIECE):
        lanes = slice(start, start + PIECE)
        rate = rate_ref[:, lanes]
        hidden = before(lanes).astype(F32)
        for t, after in ((0, middle), (1, fresh)):
            at = pl.ds(t * slots + slot, 1)
            hidden = advance(hidden, rate, size[at, lanes], drive[at, lanes], wide(b_rows[t], PIECE))
            after[place, :, lanes] = hidden.astype(BF16)


def stay_kernel(n, tps, cap, stays, step, land_tab, stay_tab, own_sum, *rest):
    got = rest[: tps - 1]
    dt_weight, dt_bias, rate_ref, conv_out, near, ssm = rest[tps - 1 : tps + 5]
    new_ssm, size_s, drive_s, b_all, c_all, c_far, middle, fresh, sems = rest[tps + 5 :]
    rank = dt_weight.shape[0]
    states, channels = rate_ref.shape
    slots = ssm.shape[0]
    far = (n - 2) * cap

    raw = own_sum[:, :rank]
    tail = own_sum[:, rank:]
    for g in got:
        raw += g[:, :rank].astype(F32)
        piece = g[:, rank:].astype(F32)
        tail += piece + pltpu.roll(piece, LANES - 2 * states, 1)
    scale = lax.rsqrt(jnp.mean(raw * raw, axis=1, keepdims=True) + 1e-06)
    normed = (raw * scale).astype(BF16)
    for start in range(0, channels, step):
        lanes = slice(start, start + step)
        pre = jnp.dot(normed, dt_weight[:, lanes], preferred_element_type=F32) + dt_bias[:, lanes]
        size = jnp.maximum(pre, 0.0) + jnp.log1p(jnp.exp(-jnp.abs(pre)))
        size_s[:, lanes] = size
        drive_s[:, lanes] = size * conv_out[:, lanes]
    b_all[...] = spread(tail, 0, states)
    col = lax.div(iota((1, slots * states), 1), states)
    far_col = lax.div(iota((1, far * states), 1), states)
    far_slot = jnp.full(far_col.shape, -1, jnp.int32)
    for i in range(far):
        far_slot = jnp.where(far_col == i, land_tab[2 * cap + i], far_slot)
    for t in range(2):
        mine = tail[t * slots : (t + 1) * slots]
        c_all[t] = spread_diagonal(mine, states, states, col)
        c_far[t] = spread_diagonal(mine, states, states, far_slot)
    for i in range(far):
        slot = jnp.maximum(land_tab[2 * cap + i], 0)
        middle[slot] = jnp.zeros((states, channels), BF16)
        fresh[slot] = jnp.zeros((states, channels), BF16)

    def store(slot, i):
        return pltpu.make_async_copy(fresh.at[slot], new_ssm.at[slot], sems.at[i])

    def update(slot, before, i):
        both_steps(slot, slots, before, slot, rate_ref, size_s, drive_s, b_all, middle, fresh)
        store(slot, i).start()

    def stay(i, _):
        slot = stay_tab[i]
        update(slot, lambda lanes: ssm[slot, :, lanes], i)
        return 0

    def arrive(i, _):
        slot = land_tab[cap + i]

        @pl.when(slot >= 0)
        def _():
            update(slot, lambda lanes: near[i, :, lanes], stays + i)

        return 0

    lax.fori_loop(0, stays, stay, 0)
    lax.fori_loop(0, cap, arrive, 0)
    for i in range(stays):
        store(stay_tab[i], i).wait()
    for i in range(cap):
        pl.when(land_tab[cap + i] >= 0)(store(land_tab[cap + i], stays + i).wait)


def arrive_kernel(n, cap, full, step, land_tab, *rest):
    far_peers = n - 2
    got = rest[:far_peers]
    rate_ref, size, drive, b_all, c_all, c_far, middle, fresh, skipped, gate, _ = rest[far_peers : far_peers + 11]
    out, new_ssm, held, mid_far, new_far, total, done_s, got_sems, sems, out_sems = rest[far_peers + 11 :]
    channels = rate_ref.shape[1]
    far = far_peers * cap
    slots = out.shape[1]
    loads = [pltpu.make_async_copy(g, held.at[at], got_sems.at[at]) for at, g in enumerate(got)]
    for load in loads:
        load.start()

    def copy(i):
        return pltpu.make_async_copy(new_far.at[i], new_ssm.at[land_tab[2 * cap + i]], sems.at[i])

    def copy_out(place):
        lanes = pl.ds(place * step, step)
        return pltpu.make_async_copy(done_s.at[:, :, lanes], out.at[:, :, lanes], out_sems.at[place])

    parts = [slice(start, start + step) for start in range(0, channels, step)]
    for lanes in parts:
        for t, after in ((0, middle), (1, fresh)):
            total[t * slots : (t + 1) * slots, lanes] = read(c_all[t], after[:, :, lanes])
    for at, load in enumerate(loads):
        load.wait()

        def one(s, _, at=at):
            i = at * cap + s
            slot = land_tab[2 * cap + i]

            def before(lanes):
                state = held[at, s, :, lanes]
                return state if far + cap == full else jnp.where(slot >= 0, state, jnp.zeros_like(state))

            both_steps(jnp.maximum(slot, 0), slots, before, i, rate_ref, size, drive, b_all, mid_far, new_far)
            pl.when(slot >= 0)(copy(i).start)
            return 0

        lax.fori_loop(0, cap, one, 0)
    for place, lanes in enumerate(parts):
        for t, after in ((0, mid_far), (1, new_far)):
            at = slice(t * slots, (t + 1) * slots)
            sums = total[at, lanes] + read(c_far[t], after[:, :, lanes])
            done_s[t, :, lanes] = ((sums + skipped[at, lanes]) * gate[at, lanes]).astype(BF16)
        copy_out(place).start()
    for place in range(len(parts)):
        copy_out(place).wait()
    for i in range(far):
        pl.when(land_tab[2 * cap + i] >= 0)(copy(i).wait)


def exchange(value, axis, k, n):
    return lax.ppermute(value, axis, [(i, i ^ k) for i in range(n)])


def cost(flops):
    return pl.CostEstimate(flops=flops, bytes_accessed=0, transcendentals=0)


def params(mib):
    return pltpu.CompilerParams(vmem_limit_bytes=mib * MIB)


def local(
    n,
    tps,
    x_new,
    z_new,
    ssm_state,
    conv_state,
    conv_weight,
    conv_bias,
    proj_weight,
    dt_weight,
    dt_bias,
    a_log,
    skip_gain,
    leave_slot,
    dest_table,
    land_slot,
):
    slots, states, channels = ssm_state.shape
    mig = leave_slot.shape[1]
    taps = conv_state.shape[1]
    rank = dt_weight.shape[0]
    peers = n - 1
    cap = max(2, (mig + n - 2) // (n - 1))
    movers = peers * cap
    stays = slots - mig
    chunks = 16 // math.gcd(16, taps * cap)
    rows = chunks * taps * cap
    width = channels // chunks
    smem = pl.BlockSpec(memory_space=pltpu.SMEM)
    vmem = pl.BlockSpec(memory_space=pltpu.VMEM)
    anywhere = pl.BlockSpec(memory_space=pl.ANY)
    hbm = pl.BlockSpec(memory_space=pltpu.HBM)
    shape = jax.ShapeDtypeStruct
    def far(value):
        return pltpu.with_memory_space_constraint(value, pltpu.HBM)

    own = lax.axis_index("inst").astype(jnp.int32).reshape(1)
    conv_t = jnp.transpose(conv_state, (1, 0, 2))
    proj_t = proj_weight.T
    cols = proj_t.shape[0]
    padded = rank + LANES
    bias_row = conv_bias.reshape(1, channels)
    dt_bias_row = dt_bias.reshape(1, channels)
    skip_row = skip_gain.reshape(1, channels)

    with jax.named_scope("gather_conv"):
        *conv_sent, near, leave_tab = pl.pallas_call(
            functools.partial(gather_conv_kernel, n, cap, chunks),
            out_shape=[shape((rows, width), BF16)] * peers
            + [shape((cap, states, channels), BF16), shape((n * cap,), jnp.int32)],
            in_specs=[smem] + [hbm] * 4,
            out_specs=[vmem] * (peers + 1) + [smem],
            scratch_shapes=[
                pltpu.SMEM(leave_slot.shape, jnp.int32),
                pltpu.SMEM(dest_table.shape, jnp.int32),
                pltpu.VMEM((taps, slots, channels), BF16),
                pltpu.SemaphoreType.DMA((chunks + 2,)),
                pltpu.SemaphoreType.DMA((1, cap)),
            ],
            compiler_params=params(16),
        )(own, far(leave_slot), far(dest_table), far(conv_t), far(ssm_state))

    order = sorted(range(1, n), key=lambda k: -k)
    conv_got, ssm_got = {}, {}
    for k in order:
        conv_got[k] = exchange(conv_sent[k - 1], "inst", k, n)
    ssm_got[1] = exchange(near, "inst", 1, n)

    far_peers = list(range(2, n))
    with jax.named_scope("gather_ssm"):
        *ssm_sent, land_tab, stay_tab = pl.pallas_call(
            functools.partial(gather_ssm_kernel, n, cap, far_peers),
            out_shape=[shape((cap, states, channels), BF16)] * len(far_peers)
            + [shape((n * cap + 1,), jnp.int32), shape((slots,), jnp.int32)],
            in_specs=[smem] * 2 + [hbm] * 4 + [anywhere],
            out_specs=[vmem] * len(far_peers) + [smem, smem],
            scratch_shapes=[
                pltpu.SMEM(leave_slot.shape, jnp.int32),
                pltpu.SMEM(dest_table.shape, jnp.int32),
                pltpu.SMEM(land_slot.shape, jnp.int32),
                pltpu.SMEM((slots,), jnp.int32),
                pltpu.SemaphoreType.DMA((len(far_peers), cap)),
                pltpu.SemaphoreType.DMA((3,)),
            ],
            compiler_params=params(16),
        )(own, leave_tab, far(leave_slot), far(dest_table), far(land_slot), far(ssm_state), conv_got[1])
    for k in reversed(far_peers):
        ssm_got[k] = exchange(ssm_sent[k - 2], "inst", k, n)

    both = 2 * slots
    with jax.named_scope("project"):
        conv_out, new_conv, own_sum, send_sum = pl.pallas_call(
            functools.partial(project_kernel, n, cap, chunks),
            out_shape=[
                shape((both, channels), F32),
                shape((taps, slots, channels), BF16),
                shape((both, padded), F32),
                shape((both, padded), BF16),
            ],
            in_specs=[smem, anywhere] + [vmem] * (peers + 5),
            out_specs=[vmem, hbm, vmem, vmem],
            scratch_shapes=[pltpu.VMEM((slots, channels), BF16), pltpu.SemaphoreType.DMA((3,))],
            compiler_params=params(20),
            cost_estimate=cost(10**12),
        )(
            land_tab,
            ssm_got[1],
            *[conv_got[k] for k in range(1, n)],
            conv_t,
            x_new,
            conv_weight,
            bias_row,
            proj_t,
        )

    sums_got = [exchange(send_sum, "tp", k, tps) for k in range(tps - 1, 0, -1)]

    with jax.named_scope("gate"):
        ssm_held, weight_held, gate, skipped, rate = pl.pallas_call(
            gate_kernel,
            out_shape=[
                shape((slots, states, channels), BF16),
                shape((rank, channels), BF16),
                shape((both, channels), F32),
                shape((both, channels), F32),
                shape((states, channels), F32),
            ],
            in_specs=[vmem] * 4 + [hbm] * 2,
            out_specs=[vmem] * 5,
            scratch_shapes=[pltpu.SemaphoreType.DMA((2,))],
            compiler_params=params(20),
        )(conv_out, z_new.reshape(both, channels), skip_row, a_log, far(ssm_state), far(dt_weight))

    step = min(1024, channels)
    far_rows = (n - 2) * cap
    with jax.named_scope("update_staying"):
        new_ssm, *state = pl.pallas_call(
            functools.partial(stay_kernel, n, tps, cap, stays, step),
            out_shape=[
                shape((slots, states, channels), BF16),
                shape((both, channels), F32),
                shape((both, channels), F32),
                shape((both, states, LANES), F32),
                shape((2, both, slots * states), BF16),
                shape((2, both, far_rows * states), BF16),
                shape((slots, states, channels), BF16),
                shape((slots, states, channels), BF16),
            ],
            in_specs=[smem, smem] + [vmem] * (tps + 6),
            out_specs=[hbm] + [vmem] * 7,
            scratch_shapes=[pltpu.SemaphoreType.DMA((stays + cap,))],
            compiler_params=params(20),
        )(
            land_tab,
            stay_tab,
            own_sum,
            *sums_got,
            weight_held,
            dt_bias_row,
            rate,
            conv_out,
            ssm_got[1],
            ssm_held,
        )

    parts = channels // step
    with jax.named_scope("update_arrived"):
        outputs, new_ssm = pl.pallas_call(
            functools.partial(arrive_kernel, n, cap, mig, step),
            out_shape=[shape((2, slots, channels), BF16), shape((slots, states, channels), BF16)],
            in_specs=[smem] + [anywhere] * (n - 2) + [vmem] * 10 + [hbm],
            out_specs=[hbm, hbm],
            scratch_shapes=[
                pltpu.VMEM((n - 2, cap, states, channels), BF16),
                pltpu.VMEM((far_rows, states, channels), BF16),
                pltpu.VMEM((far_rows, states, channels), BF16),
                pltpu.VMEM((both, channels), F32),
                pltpu.VMEM((2, slots, channels), BF16),
                pltpu.SemaphoreType.DMA((n - 2,)),
                pltpu.SemaphoreType.DMA((far_rows,)),
                pltpu.SemaphoreType.DMA((parts,)),
            ],
            input_output_aliases={1 + (n - 2) + 10: 1},
            compiler_params=params(16),
        )(land_tab, *[ssm_got[k] for k in range(2, n)], rate, *state, skipped, gate, new_ssm)
    return outputs, new_ssm, jnp.transpose(new_conv, (1, 0, 2))


def solution(mesh):
    return jax.shard_map(
        functools.partial(local, mesh.shape["inst"], mesh.shape["tp"]),
        mesh=mesh,
        in_specs=(
            P(None, ("groups", "inst"), "tp"),
            P(None, ("groups", "inst"), "tp"),
            P(("groups", "inst"), None, "tp"),
            P(("groups", "inst"), None, "tp"),
            P(None, "tp"),
            P("tp"),
            P("tp", None),
            P(None, "tp"),
            P("tp"),
            P(None, "tp"),
            P("tp"),
            P(("groups", "inst"), None),
            P("groups", None),
            P(("groups", "inst"), None),
        ),
        out_specs=(
            P(None, ("groups", "inst"), "tp"),
            P(("groups", "inst"), None, "tp"),
            P(("groups", "inst"), None, "tp"),
        ),
        check_vma=False,
    )
```

```python
import functools
import math

import jax
import jax.numpy as jnp
from jax import lax
from jax.experimental import pallas as pl
from jax.experimental.pallas import tpu as pltpu
from jax.sharding import PartitionSpec as P

F32 = jnp.float32
BF16 = jnp.bfloat16
LANES = 128
LOG2E = math.log2(math.e)
MIB = 1 << 20
PIECE = 512
PACK = 16


def iota(shape, dim):
    return lax.broadcasted_iota(jnp.int32, shape, dim)


def silu(value):
    return value / (1.0 + jnp.exp(-value))


def gather_conv_kernel(n, cap, chunks, own_ref, leave_hbm, dest_hbm, conv_hbm, ssm, *rest):
    peers = n - 1
    send = rest[:peers]
    near, leave_tab, leave, dest, conv, sems, row_sems = rest[peers:]
    mig = leave.shape[1]
    taps, slots, channels = conv.shape
    width = channels // chunks
    own = own_ref[0]
    tables = [
        pltpu.make_async_copy(leave_hbm, leave, sems.at[chunks]),
        pltpu.make_async_copy(dest_hbm, dest, sems.at[chunks + 1]),
    ]
    for table in tables:
        table.start()
    loads = []
    for q in range(chunks):
        lanes = pl.ds(q * width, width)
        loads.append(pltpu.make_async_copy(conv_hbm.at[:, :, lanes], conv.at[:, :, lanes], sems.at[q]))
        loads[q].start()
    for i in range(n * cap):
        leave_tab[i] = -1
    for table in tables:
        table.wait()
    away = [dest[own, pos] ^ own for pos in range(mig)]
    for pos in range(mig):
        place = 0
        for earlier in range(pos):
            place = place + jnp.where(away[earlier] == away[pos], 1, 0)
        leave_tab[away[pos] * cap + place] = leave[0, pos]
    pairs = row_copies(ssm, [near], row_sems, leave_tab, cap, [1])
    start_all(pairs)

    rows = chunks * taps * cap
    row = iota((peers * rows, 1), 0)
    inner = lax.rem(row, rows)
    place = lax.rem(inner, cap)
    tap = lax.rem(lax.div(inner, cap), taps)
    chunk = lax.div(inner, taps * cap)
    peer = lax.div(row, rows)
    source = jnp.full(row.shape, -1, jnp.int32)
    for k in range(1, n):
        for s in range(cap):
            slot = leave_tab[k * cap + s]
            source = jnp.where((peer == k - 1) & (place == s) & (slot >= 0), tap * slots + slot, source)
    pick = jnp.where(source == iota((peers * rows, taps * slots), 1), 1.0, 0.0)
    total = None
    for q in range(chunks):
        loads[q].wait()
        part = jnp.dot(
            jnp.where(chunk == q, pick, 0.0).astype(BF16),
            conv[:, :, q * width : (q + 1) * width].reshape(taps * slots, width),
            preferred_element_type=F32,
        )
        total = part if total is None else total + part
    for k in range(1, n):
        send[k - 1][...] = total[(k - 1) * rows : k * rows, :].astype(BF16)
    wait_all(pairs)


def row_copies(ssm, send, sems, tab, cap, peer_list):
    pairs = []
    for at, k in enumerate(peer_list):
        for s in range(cap):
            slot = tab[k * cap + s]
            pairs.append((slot >= 0, pltpu.make_async_copy(ssm.at[slot], send[at].at[s], sems.at[at, s])))
    return pairs


def start_all(pairs):
    for present, copy in pairs:
        pl.when(present)(copy.start)


def wait_all(pairs):
    for present, copy in pairs:
        pl.when(present)(copy.wait)


def gather_ssm_kernel(n, cap, peer_list, own_ref, leave_tab, leave_hbm, dest_hbm, land_hbm, ssm, _, *rest):
    send = rest[: len(peer_list)]
    land_tab, stay_tab, leave, dest, land, flags, sems, table_sems = rest[len(peer_list) :]
    mig = leave.shape[1]
    slots = ssm.shape[0]
    own = own_ref[0]
    tables = [
        pltpu.make_async_copy(source, target, table_sems.at[i])
        for i, (source, target) in enumerate(((leave_hbm, leave), (dest_hbm, dest), (land_hbm, land)))
    ]
    for table in tables:
        table.start()
    pairs = row_copies(ssm, send, sems, leave_tab, cap, peer_list)
    start_all(pairs)
    for i in range(n * cap + 1):
        land_tab[i] = -1
    for i in range(slots):
        flags[i] = 0
    for table in tables:
        table.wait()

    def arrivals(source, rank):
        base = (source ^ own) * cap
        place = 0
        for pos in range(mig):
            hit = jnp.where(dest[source, pos] == own, 1, 0)
            land_tab[jnp.where(hit == 1, base + place, n * cap)] = land[0, jnp.minimum(rank, mig - 1)]
            rank, place = rank + hit, place + hit
        return rank

    if n <= 4:
        rank = 0
        for source in range(n):
            rank = arrivals(source, rank)
    else:
        lax.fori_loop(0, n, arrivals, 0)
    for pos in range(mig):
        flags[leave[0, pos]] = 1
    count = 0
    for slot in range(slots):
        stay_tab[count] = slot
        count = count + 1 - flags[slot]
    wait_all(pairs)


def project_kernel(n, cap, chunks, land_tab, _, *rest):
    peers = n - 1
    got = rest[:peers]
    conv, x_new, weight, bias, proj = rest[peers : peers + 5]
    conv_out, new_conv, own_sum, send_sum, newest, sems = rest[peers + 5 :]
    taps, slots, channels = conv.shape
    width = channels // chunks
    rows = got[0].shape[0]
    cols = proj.shape[0]
    store = [pltpu.make_async_copy(x_new.at[t], new_conv.at[taps - 2 + t], sems.at[t]) for t in range(2)]
    store.append(pltpu.make_async_copy(newest, new_conv.at[0], sems.at[2]))
    store[0].start()
    store[1].start()

    col = iota((1, peers * rows), 1)
    inner = lax.rem(col, rows)
    target = jnp.full(col.shape, -1, jnp.int32)
    slot_row = iota((slots, 1), 0)
    arrived = jnp.zeros((slots, 1), jnp.bool_)
    for k in range(1, n):
        for s in range(cap):
            slot = land_tab[k * cap + s]
            target = jnp.where((lax.div(col, rows) == k - 1) & (lax.rem(inner, cap) == s), slot, target)
            arrived = arrived | (slot_row == slot)
    tap = lax.rem(lax.div(inner, cap), taps)
    chunk = lax.div(inner, taps * cap)
    target = jnp.where(target >= 0, tap * slots + target, -1)
    grid_row = iota((taps * slots, peers * rows), 0)
    incoming = jnp.concatenate([g[...] for g in got], axis=0)
    total = jnp.zeros((2 * slots, cols), F32)
    for q in range(chunks):
        lanes = slice(q * width, (q + 1) * width)
        pick = jnp.where(grid_row == jnp.where(chunk == q, target, -1), 1.0, 0.0).astype(BF16)
        moved = jnp.dot(pick, incoming, preferred_element_type=F32)
        history = [
            jnp.where(arrived, moved[j * slots : (j + 1) * slots], conv[j, :, lanes].astype(F32)) for j in range(taps)
        ]
        newest[:, lanes] = history[taps - 1].astype(BF16)
        window = history + [x_new[t, :, lanes].astype(F32) for t in range(2)]
        halves = []
        for t in range(2):
            value = window[t] * weight[0:1, lanes]
            for j in range(1, taps + 1):
                value += window[t + j] * weight[j : j + 1, lanes]
            value = silu(value + bias[:, lanes])
            conv_out[t * slots : (t + 1) * slots, lanes] = value
            halves.append(value.astype(BF16))
        total += lax.dot_general(
            jnp.concatenate(halves, axis=0),
            proj[:, lanes],
            (((1,), (1,)), ((), ())),
            preferred_element_type=F32,
        )
    store[2].start()
    rank = own_sum.shape[1] - LANES
    own_sum[:, rank:] = jnp.zeros((2 * slots, LANES), F32)
    own_sum[:, :cols] = total
    tail = own_sum[:, rank:]
    send_sum[: 2 * slots, :] = total[:, :rank].astype(BF16)
    high = tail.astype(BF16).astype(F32)
    used = cols - rank
    pair = high + pltpu.roll(tail - high, used, 1)
    packed = pair[:slots] + pltpu.roll(pair[slots:], 2 * used, 1)
    send_sum[2 * slots :, :] = jnp.zeros((PACK, rank), BF16)
    for at in range(slots // PACK):
        block = packed[at * PACK : (at + 1) * PACK]
        send_sum[2 * slots :, at * LANES : (at + 1) * LANES] = block.astype(BF16)
    for copy in store:
        copy.wait()


def spread(values, lane, states):
    rows = values.shape[0]
    wide = jnp.broadcast_to(values[:, None, :], (rows, states, LANES))
    keep = iota(wide.shape, 2) == iota(wide.shape, 1) + lane
    wide = jnp.where(keep, wide, 0.0).reshape(rows * states, LANES)
    high = wide.astype(BF16)
    low = (wide - high.astype(F32)).astype(BF16)
    ones = jnp.ones((LANES, LANES), BF16)
    both = jnp.dot(high, ones, preferred_element_type=F32) + jnp.dot(low, ones, preferred_element_type=F32)
    return both.reshape(rows, states, LANES)


def spread_diagonal(values, lane, states, owner):
    cols = owner.shape[1]
    pick = iota((LANES, cols), 0) == lax.rem(iota((LANES, cols), 1), states) + lane
    pick = jnp.where(pick, 1.0, 0.0).astype(BF16)
    keep = owner == iota((values.shape[0], cols), 0)
    high = values.astype(BF16)
    low = (values - high.astype(F32)).astype(BF16)
    parts = [jnp.where(keep, jnp.dot(v, pick, preferred_element_type=F32), 0.0) for v in (high, low)]
    return jnp.concatenate(parts, axis=0).astype(BF16)


def read(weights, hidden):
    both = jnp.dot(weights, hidden.reshape(-1, hidden.shape[2]), preferred_element_type=F32)
    half = both.shape[0] // 2
    return both[:half] + both[half:]


def advance(hidden, rate, size, drive, b_part):
    return jnp.exp2(size * rate) * hidden + drive * b_part


def wide(tile, lanes):
    return jnp.concatenate([tile] * (lanes // LANES), axis=1)


def gate_kernel(conv_out, z_new, skip, a_log, ssm, dt_weight, ssm_held, weight_held, gate, skipped, rate, sems):
    held = [
        pltpu.make_async_copy(ssm, ssm_held, sems.at[0]),
        pltpu.make_async_copy(dt_weight, weight_held, sems.at[1]),
    ]
    for copy in held:
        copy.start()
    gate[...] = silu(z_new[...].astype(F32))
    skipped[...] = skip[...] * conv_out[...]
    rate[...] = -LOG2E * jnp.exp(a_log[...])
    for copy in held:
        copy.wait()


def both_steps(slot, slots, before, place, rate_ref, size, drive, b_all, middle, fresh):
    b_rows = [b_all[t * slots + slot] for t in range(2)]
    for start in range(0, rate_ref.shape[1], PIECE):
        lanes = slice(start, start + PIECE)
        rate = rate_ref[:, lanes]
        hidden = before(lanes).astype(F32)
        for t, after in ((0, middle), (1, fresh)):
            at = pl.ds(t * slots + slot, 1)
            hidden = advance(hidden, rate, size[at, lanes], drive[at, lanes], wide(b_rows[t], PIECE))
            after[place, :, lanes] = hidden.astype(BF16)


def stay_kernel(n, tps, cap, stays, step, land_tab, stay_tab, own_sum, *rest):
    got = rest[: tps - 1]
    dt_weight, dt_bias, rate_ref, conv_out, near, ssm = rest[tps - 1 : tps + 5]
    new_ssm, size_s, drive_s, b_all, c_all, c_far, middle, fresh, sems = rest[tps + 5 :]
    rank = dt_weight.shape[0]
    states, channels = rate_ref.shape
    slots = ssm.shape[0]
    far = (n - 2) * cap

    raw = own_sum[:, :rank]
    tail = own_sum[:, rank:]
    used = 2 * states
    for g in got:
        raw += g[: 2 * slots, :].astype(F32)
        blocks = [g[2 * slots :, at * LANES : (at + 1) * LANES] for at in range(slots // PACK)]
        pair = jnp.concatenate(blocks, axis=0).astype(F32)
        pair += pltpu.roll(pair, LANES - used, 1)
        tail += jnp.concatenate([pair, pltpu.roll(pair, LANES - 2 * used, 1)], axis=0)
    scale = lax.rsqrt(jnp.mean(raw * raw, axis=1, keepdims=True) + 1e-06)
    normed = (raw * scale).astype(BF16)
    for start in range(0, channels, step):
        lanes = slice(start, start + step)
        pre = jnp.dot(normed, dt_weight[:, lanes], preferred_element_type=F32) + dt_bias[:, lanes]
        size = jnp.maximum(pre, 0.0) + jnp.log1p(jnp.exp(-jnp.abs(pre)))
        size_s[:, lanes] = size
        drive_s[:, lanes] = size * conv_out[:, lanes]
    b_all[...] = spread(tail, 0, states)
    col = lax.div(iota((1, slots * states), 1), states)
    far_col = lax.div(iota((1, far * states), 1), states)
    far_slot = jnp.full(far_col.shape, -1, jnp.int32)
    for i in range(far):
        far_slot = jnp.where(far_col == i, land_tab[2 * cap + i], far_slot)
    for t in range(2):
        mine = tail[t * slots : (t + 1) * slots]
        c_all[t] = spread_diagonal(mine, states, states, col)
        c_far[t] = spread_diagonal(mine, states, states, far_slot)
    for i in range(far):
        slot = jnp.maximum(land_tab[2 * cap + i], 0)
        middle[slot] = jnp.zeros((states, channels), BF16)
        fresh[slot] = jnp.zeros((states, channels), BF16)

    def store(slot, i):
        return pltpu.make_async_copy(fresh.at[slot], new_ssm.at[slot], sems.at[i])

    def update(slot, before, i):
        both_steps(slot, slots, before, slot, rate_ref, size_s, drive_s, b_all, middle, fresh)
        store(slot, i).start()

    def stay(i, _):
        slot = stay_tab[i]
        update(slot, lambda lanes: ssm[slot, :, lanes], i)
        return 0

    def arrive(i, _):
        slot = land_tab[cap + i]

        @pl.when(slot >= 0)
        def _():
            update(slot, lambda lanes: near[i, :, lanes], stays + i)

        return 0

    lax.fori_loop(0, stays, stay, 0)
    lax.fori_loop(0, cap, arrive, 0)
    for i in range(stays):
        store(stay_tab[i], i).wait()
    for i in range(cap):
        pl.when(land_tab[cap + i] >= 0)(store(land_tab[cap + i], stays + i).wait)


def arrive_kernel(n, cap, full, step, land_tab, *rest):
    far_peers = n - 2
    got = rest[:far_peers]
    rate_ref, size, drive, b_all, c_all, c_far, middle, fresh, skipped, gate, _ = rest[far_peers : far_peers + 11]
    out, new_ssm, held, mid_far, new_far, total, done_s, got_sems, sems, out_sems = rest[far_peers + 11 :]
    channels = rate_ref.shape[1]
    far = far_peers * cap
    slots = out.shape[1]
    loads = [pltpu.make_async_copy(g, held.at[at], got_sems.at[at]) for at, g in enumerate(got)]
    for load in loads:
        load.start()

    def copy(i):
        return pltpu.make_async_copy(new_far.at[i], new_ssm.at[land_tab[2 * cap + i]], sems.at[i])

    def copy_out(place):
        lanes = pl.ds(place * step, step)
        return pltpu.make_async_copy(done_s.at[:, :, lanes], out.at[:, :, lanes], out_sems.at[place])

    parts = [slice(start, start + step) for start in range(0, channels, step)]
    for lanes in parts:
        for t, after in ((0, middle), (1, fresh)):
            total[t * slots : (t + 1) * slots, lanes] = read(c_all[t], after[:, :, lanes])
    for at, load in enumerate(loads):
        load.wait()

        def one(s, _, at=at):
            i = at * cap + s
            slot = land_tab[2 * cap + i]

            def before(lanes):
                state = held[at, s, :, lanes]
                return state if far + cap == full else jnp.where(slot >= 0, state, jnp.zeros_like(state))

            both_steps(jnp.maximum(slot, 0), slots, before, i, rate_ref, size, drive, b_all, mid_far, new_far)
            pl.when(slot >= 0)(copy(i).start)
            return 0

        lax.fori_loop(0, cap, one, 0)
    for place, lanes in enumerate(parts):
        for t, after in ((0, mid_far), (1, new_far)):
            at = slice(t * slots, (t + 1) * slots)
            sums = total[at, lanes] + read(c_far[t], after[:, :, lanes])
            done_s[t, :, lanes] = ((sums + skipped[at, lanes]) * gate[at, lanes]).astype(BF16)
        copy_out(place).start()
    for place in range(len(parts)):
        copy_out(place).wait()
    for i in range(far):
        pl.when(land_tab[2 * cap + i] >= 0)(copy(i).wait)


def exchange(value, axis, k, n):
    return lax.ppermute(value, axis, [(i, i ^ k) for i in range(n)])


def cost(flops):
    return pl.CostEstimate(flops=flops, bytes_accessed=0, transcendentals=0)


def params(mib):
    return pltpu.CompilerParams(vmem_limit_bytes=mib * MIB)


def local(
    n,
    tps,
    x_new,
    z_new,
    ssm_state,
    conv_state,
    conv_weight,
    conv_bias,
    proj_weight,
    dt_weight,
    dt_bias,
    a_log,
    skip_gain,
    leave_slot,
    dest_table,
    land_slot,
):
    slots, states, channels = ssm_state.shape
    mig = leave_slot.shape[1]
    taps = conv_state.shape[1]
    rank = dt_weight.shape[0]
    peers = n - 1
    cap = max(2, (mig + n - 2) // (n - 1))
    movers = peers * cap
    stays = slots - mig
    chunks = 16 // math.gcd(16, taps * cap)
    rows = chunks * taps * cap
    width = channels // chunks
    smem = pl.BlockSpec(memory_space=pltpu.SMEM)
    vmem = pl.BlockSpec(memory_space=pltpu.VMEM)
    anywhere = pl.BlockSpec(memory_space=pl.ANY)
    hbm = pl.BlockSpec(memory_space=pltpu.HBM)
    shape = jax.ShapeDtypeStruct
    def far(value):
        return pltpu.with_memory_space_constraint(value, pltpu.HBM)

    own = lax.axis_index("inst").astype(jnp.int32).reshape(1)
    conv_t = jnp.transpose(conv_state, (1, 0, 2))
    proj_t = proj_weight.T
    cols = proj_t.shape[0]
    padded = rank + LANES
    bias_row = conv_bias.reshape(1, channels)
    dt_bias_row = dt_bias.reshape(1, channels)
    skip_row = skip_gain.reshape(1, channels)

    with jax.named_scope("gather_conv"):
        *conv_sent, near, leave_tab = pl.pallas_call(
            functools.partial(gather_conv_kernel, n, cap, chunks),
            out_shape=[shape((rows, width), BF16)] * peers
            + [shape((cap, states, channels), BF16), shape((n * cap,), jnp.int32)],
            in_specs=[smem] + [hbm] * 4,
            out_specs=[vmem] * (peers + 1) + [smem],
            scratch_shapes=[
                pltpu.SMEM(leave_slot.shape, jnp.int32),
                pltpu.SMEM(dest_table.shape, jnp.int32),
                pltpu.VMEM((taps, slots, channels), BF16),
                pltpu.SemaphoreType.DMA((chunks + 2,)),
                pltpu.SemaphoreType.DMA((1, cap)),
            ],
            compiler_params=params(16),
        )(own, far(leave_slot), far(dest_table), far(conv_t), far(ssm_state))

    order = sorted(range(1, n), key=lambda k: -k)
    conv_got, ssm_got = {}, {}
    for k in order:
        conv_got[k] = exchange(conv_sent[k - 1], "inst", k, n)
    ssm_got[1] = exchange(near, "inst", 1, n)

    far_peers = list(range(2, n))
    with jax.named_scope("gather_ssm"):
        *ssm_sent, land_tab, stay_tab = pl.pallas_call(
            functools.partial(gather_ssm_kernel, n, cap, far_peers),
            out_shape=[shape((cap, states, channels), BF16)] * len(far_peers)
            + [shape((n * cap + 1,), jnp.int32), shape((slots,), jnp.int32)],
            in_specs=[smem] * 2 + [hbm] * 4 + [anywhere],
            out_specs=[vmem] * len(far_peers) + [smem, smem],
            scratch_shapes=[
                pltpu.SMEM(leave_slot.shape, jnp.int32),
                pltpu.SMEM(dest_table.shape, jnp.int32),
                pltpu.SMEM(land_slot.shape, jnp.int32),
                pltpu.SMEM((slots,), jnp.int32),
                pltpu.SemaphoreType.DMA((len(far_peers), cap)),
                pltpu.SemaphoreType.DMA((3,)),
            ],
            compiler_params=params(16),
        )(own, leave_tab, far(leave_slot), far(dest_table), far(land_slot), far(ssm_state), conv_got[1])
    for k in reversed(far_peers):
        ssm_got[k] = exchange(ssm_sent[k - 2], "inst", k, n)

    both = 2 * slots
    with jax.named_scope("project"):
        conv_out, new_conv, own_sum, send_sum = pl.pallas_call(
            functools.partial(project_kernel, n, cap, chunks),
            out_shape=[
                shape((both, channels), F32),
                shape((taps, slots, channels), BF16),
                shape((both, padded), F32),
                shape((both + PACK, rank), BF16),
            ],
            in_specs=[smem, anywhere] + [vmem] * (peers + 5),
            out_specs=[vmem, hbm, vmem, vmem],
            scratch_shapes=[pltpu.VMEM((slots, channels), BF16), pltpu.SemaphoreType.DMA((3,))],
            compiler_params=params(20),
            cost_estimate=cost(10**12),
        )(
            land_tab,
            ssm_got[1],
            *[conv_got[k] for k in range(1, n)],
            conv_t,
            x_new,
            conv_weight,
            bias_row,
            proj_t,
        )

    sums_got = [exchange(send_sum, "tp", k, tps) for k in range(1, tps)]

    with jax.named_scope("gate"):
        ssm_held, weight_held, gate, skipped, rate = pl.pallas_call(
            gate_kernel,
            out_shape=[
                shape((slots, states, channels), BF16),
                shape((rank, channels), BF16),
                shape((both, channels), F32),
                shape((both, channels), F32),
                shape((states, channels), F32),
            ],
            in_specs=[vmem] * 4 + [hbm] * 2,
            out_specs=[vmem] * 5,
            scratch_shapes=[pltpu.SemaphoreType.DMA((2,))],
            compiler_params=params(20),
        )(conv_out, z_new.reshape(both, channels), skip_row, a_log, far(ssm_state), far(dt_weight))

    step = min(1024, channels)
    far_rows = (n - 2) * cap
    with jax.named_scope("update_staying"):
        new_ssm, *state = pl.pallas_call(
            functools.partial(stay_kernel, n, tps, cap, stays, step),
            out_shape=[
                shape((slots, states, channels), BF16),
                shape((both, channels), F32),
                shape((both, channels), F32),
                shape((both, states, LANES), F32),
                shape((2, both, slots * states), BF16),
                shape((2, both, far_rows * states), BF16),
                shape((slots, states, channels), BF16),
                shape((slots, states, channels), BF16),
            ],
            in_specs=[smem, smem] + [vmem] * (tps + 6),
            out_specs=[hbm] + [vmem] * 7,
            scratch_shapes=[pltpu.SemaphoreType.DMA((stays + cap,))],
            compiler_params=params(20),
        )(
            land_tab,
            stay_tab,
            own_sum,
            *sums_got,
            weight_held,
            dt_bias_row,
            rate,
            conv_out,
            ssm_got[1],
            ssm_held,
        )

    parts = channels // step
    with jax.named_scope("update_arrived"):
        outputs, new_ssm = pl.pallas_call(
            functools.partial(arrive_kernel, n, cap, mig, step),
            out_shape=[shape((2, slots, channels), BF16), shape((slots, states, channels), BF16)],
            in_specs=[smem] + [anywhere] * (n - 2) + [vmem] * 10 + [hbm],
            out_specs=[hbm, hbm],
            scratch_shapes=[
                pltpu.VMEM((n - 2, cap, states, channels), BF16),
                pltpu.VMEM((far_rows, states, channels), BF16),
                pltpu.VMEM((far_rows, states, channels), BF16),
                pltpu.VMEM((both, channels), F32),
                pltpu.VMEM((2, slots, channels), BF16),
                pltpu.SemaphoreType.DMA((n - 2,)),
                pltpu.SemaphoreType.DMA((far_rows,)),
                pltpu.SemaphoreType.DMA((parts,)),
            ],
            input_output_aliases={1 + (n - 2) + 10: 1},
            compiler_params=params(16),
        )(land_tab, *[ssm_got[k] for k in range(2, n)], rate, *state, skipped, gate, new_ssm)
    return outputs, new_ssm, jnp.transpose(new_conv, (1, 0, 2))


def solution(mesh):
    return jax.shard_map(
        functools.partial(local, mesh.shape["inst"], mesh.shape["tp"]),
        mesh=mesh,
        in_specs=(
            P(None, ("groups", "inst"), "tp"),
            P(None, ("groups", "inst"), "tp"),
            P(("groups", "inst"), None, "tp"),
            P(("groups", "inst"), None, "tp"),
            P(None, "tp"),
            P("tp"),
            P("tp", None),
            P(None, "tp"),
            P("tp"),
            P(None, "tp"),
            P("tp"),
            P(("groups", "inst"), None),
            P("groups", None),
            P(("groups", "inst"), None),
        ),
        out_specs=(
            P(None, ("groups", "inst"), "tp"),
            P(("groups", "inst"), None, "tp"),
            P(("groups", "inst"), None, "tp"),
        ),
        check_vma=False,
    )
```
